256 devices in a mesh: seq: 64 (over x_lo, z, y), ch: 4 (over x_hi, core).
Axes of the slice: x: 4 (x_hi: 2, x_lo: 2; x = x_hi * 2 + x_lo), y: 4, z: 8, core: 2. Of those that a mesh axis runs over, the one named last changes fastest.
Arguments:
- tokens: bfloat16 [32768, 1024], P('seq', 'ch'), may hold values from -400 to 400
- norm_gain: float32 [1024], replicated, may hold values from 0.5 to 1.5
- w_in: bfloat16 [1024, 3, 1024], P(None, None, 'ch'), may hold values from -0.1875 to 0.1875
- short_filter: float32 [3, 3, 1024], P(None, None, 'ch'), may hold values from -3 to 3
- rates: float32 [16, 1024], P(None, 'ch'), may hold values from 7.6293945e-06 to 0.05
- residues: float32 [16, 1024], P(None, 'ch'), may hold values from -1.5 to 1.5
- skip_gain: float32 [1024], P('ch'), may hold values from -4 to 4
- w_out: bfloat16 [1024, 1024], P('ch'), may hold values from -0.1875 to 0.1875
Outputs:
- mixed: bfloat16 [32768, 1024], P('seq', 'ch')
The draws below stay inside these ranges and needn't reach their ends.
All inputs are finite; a program needn't handle non-finite values.
Results may differ from the reference program's by a relative error of at most 0.009.
Values may be sent and summed in bfloat16 or wider, within the bound.
No kernel may reach another device: no remote copies, remote signals or barrier semaphores. Data moves between devices by JAX's collectives and lax.ppermute only.
A program may use at most 64 MiB of HBM per device.

```python
import math
import jax
import jax.numpy as jnp
from jax import lax

SLAB = 1024
MODES = 16
SHORT = 3
SEQ = 32768


def draw_tokens(key, part):
    key = jax.random.fold_in(key, 11)
    row_key = jax.random.fold_in(key, 0)
    col_key = jax.random.fold_in(key, 1)
    base_key = jax.random.fold_in(key, 3)
    row_scale = jnp.exp(jax.random.uniform(row_key, (SEQ, 1), jnp.float32, 0.0, math.log(10.0)))
    col_scale = jnp.exp(jax.random.uniform(col_key, (1, SLAB), jnp.float32, 0.0, math.log(10.0)))
    base_values = jnp.clip(jax.random.normal(base_key, (SEQ, SLAB), jnp.float32), -4.0, 4.0)
    return (base_values * row_scale * col_scale).astype(jnp.bfloat16)


def draw_rates(key, part):
    key = jax.random.fold_in(key, 23)
    slow_key, fast_key, pick_key = jax.random.split(key, 3)
    slow_rates = jnp.exp(jax.random.uniform(slow_key, (MODES, SLAB), jnp.float32, math.log(0.25 / SEQ), math.log(2.0 / SEQ)))
    fast_rates = jnp.exp(jax.random.uniform(fast_key, (MODES, SLAB), jnp.float32, math.log(2.0 / SEQ), math.log(0.05)))
    slow_share = 0.5
    chosen = jax.random.uniform(pick_key, (MODES, SLAB), jnp.float32) < slow_share
    return jnp.where(chosen, slow_rates, fast_rates).astype(jnp.float32)


def block_levels(key, dims, pieces, smallest, largest):
    level = 1.0
    for axis_at, parts in pieces:
        steps = jax.random.uniform(jax.random.fold_in(jax.random.fold_in(key, 6), axis_at), (parts,), jnp.float32, smallest / len(pieces), largest / len(pieces))
        level = level * jnp.repeat(jnp.exp(steps), dims[axis_at] // parts).reshape((-1,) + (1,) * (len(dims) - 1 - axis_at))
    return level


def bell_draw(key, extent, width, limit, cuts=(), kind=jnp.bfloat16):
    result = width * jax.random.normal(key, extent, jnp.float32)
    if cuts:
        result = result * block_levels(key, extent, cuts, -0.22, 0.18)
    return jnp.clip(result, -limit, limit).astype(kind)


def setup_inputs(seed: int = 0) -> dict:
    keys = jax.random.split(jax.random.key(seed), 9)
    return {
        "tokens": draw_tokens(jax.random.fold_in(keys[8], 71), 0),
        "norm_gain": jnp.clip(1.0 + 0.1 * jax.random.normal(keys[1], (SLAB,), jnp.float32), 0.5, 1.5),
        "w_in": bell_draw(keys[2], (SLAB, 3, SLAB), SLAB ** -0.5, 0.1875, ((2, 4),)),
        "short_filter": bell_draw(keys[3], (SHORT, 3, SLAB), 0.6, 3.0, ((2, 4),), jnp.float32),
        "rates": draw_rates(jax.random.fold_in(keys[8], 71), 0),
        "residues": bell_draw(keys[5], (MODES, SLAB), 0.25, 1.5, ((1, 4),), jnp.float32),
        "skip_gain": bell_draw(keys[6], (SLAB,), 1.0, 4.0, ((0, 4),), jnp.float32),
        "w_out": bell_draw(keys[7], (SLAB, SLAB), SLAB ** -0.5, 0.1875, ((0, 4),)),
    }


EPSILON = 1e-06

def block_convolve(operands):
    signal, kernel = operands
    padded_len = 2 * signal.shape[0]
    spectrum = jnp.fft.rfft(signal, n=padded_len, axis=0) * jnp.fft.rfft(kernel, n=padded_len, axis=0)
    return jnp.fft.irfft(spectrum, n=padded_len, axis=0)[:signal.shape[0]]

def reference(tokens, norm_gain, w_in, short_filter, rates, residues, skip_gain, w_out):
    values = tokens.astype(jnp.float32)
    mean_square = lax.optimization_barrier(jnp.mean(values * values, axis=-1, keepdims=True))
    normed = (values * lax.rsqrt(mean_square + EPSILON) * norm_gain).astype(jnp.bfloat16)
    projected = jnp.dot(normed, w_in.reshape(SLAB, 3 * SLAB), preferred_element_type=jnp.float32).astype(jnp.bfloat16)
    projected = projected.reshape(SEQ, 3, SLAB).astype(jnp.float32)
    padded = jnp.concatenate([jnp.zeros((SHORT - 1, 3, SLAB), jnp.float32), projected], axis=0)
    filtered = jnp.zeros((SEQ, 3, SLAB), jnp.float32)
    for tap_index in range(SHORT):
        start_row = SHORT - 1 - tap_index
        filtered = filtered + short_filter[tap_index] * padded[start_row:start_row + SEQ]
    queries = filtered[:, 0]
    gated_product = filtered[:, 1] * filtered[:, 2]
    positions = jnp.arange(SEQ).astype(jnp.float32)[:, None]
    kernel = jnp.zeros((SEQ, SLAB), jnp.float32)
    for mode_index in range(MODES):
        kernel = kernel + residues[mode_index] * jnp.sqrt(rates[mode_index]) * jnp.exp(-rates[mode_index] * positions)
    block_width = min(SLAB, 128)
    groups = SLAB // block_width
    stacked = (gated_product.reshape(SEQ, groups, block_width).transpose(1, 0, 2), kernel.reshape(SEQ, groups, block_width).transpose(1, 0, 2))
    convolved = lax.map(block_convolve, stacked).transpose(1, 0, 2).reshape(SEQ, SLAB)
    mixed_in = (queries * (convolved + skip_gain * gated_product)).astype(jnp.bfloat16)
    return jnp.dot(mixed_in, w_out, preferred_element_type=jnp.float32).astype(jnp.bfloat16)
```

```python
import functools

import jax
import jax.numpy as jnp
from jax import lax
from jax.experimental import pallas as pl
from jax.experimental.pallas import tpu as pltpu
from jax.sharding import PartitionSpec as P

EPSILON = 1e-06
F32 = jnp.float32
BF16 = jnp.bfloat16
LANES = 128
SUBS = 8
HALO = 16
VMEM_LIMIT = 48 * 1024 * 1024

SCAN_MASKS = (1, 3, 4, 8, 24, 32)


def ch_swap(array, mask):
    return lax.ppermute(array, "ch", [(i, i ^ mask) for i in range(lax.axis_size("ch"))])


def seq_swap(array, mask):
    return lax.ppermute(array, "seq", [(i, i ^ mask) for i in range(lax.axis_size("seq"))])


def vmem_specs(count):
    return [pl.BlockSpec(memory_space=pltpu.VMEM)] * count


def row(ref, index, lanes):
    return jnp.broadcast_to(ref[pl.ds(index, 1), lanes], (SUBS, LANES))


def front_kernel(
    own, far, side, side_far, halo, gain, w_in, taps, rates, residues, skip,
    queries, local, carry, ends, projected,
):
    me = lax.axis_index("ch")
    rows = own.shape[0]
    width = own.shape[1]
    span = rows // SUBS
    modes = rates.shape[0]
    blocks = [jnp.concatenate([halo[i], block[...]], axis=0) for i, block in enumerate((own, side, far, side_far))]
    square = jnp.zeros((rows + HALO, LANES), F32)
    for block in blocks:
        for lane in range(0, width, LANES):
            piece = block[:, lane : lane + LANES].astype(F32)
            square = square + piece * piece
    scale = lax.rsqrt(jnp.sum(square, axis=1, keepdims=True) * (1.0 / (4 * width)) + EPSILON)
    total = jnp.zeros((rows + HALO, w_in.shape[1]), F32)
    for order, block in enumerate(blocks):
        part = jnp.bitwise_xor(me, order)
        normed = (block.astype(F32) * scale * gain[pl.ds(part, 1), :]).astype(BF16)
        start = pl.multiple_of(part * width, width)
        total = total + jnp.dot(normed, w_in[pl.ds(start, width), :], preferred_element_type=F32)
    total = total.astype(BF16).astype(F32)
    for tile in range(total.shape[1] // LANES):
        projected[tile] = total[:, tile * LANES : (tile + 1) * LANES]

    sub = lax.broadcasted_iota(jnp.int32, (SUBS, LANES), 0)
    for lane in range(0, width, LANES):
        lanes = pl.ds(lane, LANES)
        rate = [row(rates, m, lanes) for m in range(modes)]
        decay = [jnp.exp(-r) for r in rate]
        weight = [row(residues, m, lanes) * jnp.sqrt(rate[m]) for m in range(modes)]
        tap = [[row(taps, 3 * s + g, lanes) for s in range(3)] for g in range(3)]
        skip_row = row(skip, 0, lanes)

        def read(start, group):
            return projected[(group * width + lane) // LANES, pl.ds(start, SUBS, stride=span), :]

        def step(index, held):
            before, state = held
            now = [read(HALO + index, g) for g in range(3)]
            filtered = [
                tap[g][0] * now[g] + tap[g][1] * before[0][g] + tap[g][2] * before[1][g] for g in range(3)
            ]
            gated = filtered[1] * filtered[2]
            state = [decay[m] * state[m] + gated for m in range(modes)]
            terms = [weight[m] * state[m] for m in range(modes)] + [skip_row * gated]
            while len(terms) > 1:
                terms = [sum(terms[i : i + 2][1:], terms[i]) for i in range(0, len(terms), 2)]
            at = pl.ds(pl.multiple_of(index * SUBS, SUBS), SUBS)
            queries[at, lanes] = filtered[0]
            local[at, lanes] = terms[0]
            return ((now, before[0]), state)

        first = ([read(HALO - 1, g) for g in range(3)], [read(HALO - 2, g) for g in range(3)])
        zeros = [jnp.zeros((SUBS, LANES), F32)] * modes
        _, state = lax.fori_loop(0, span, step, (first, zeros), unroll=4)
        for m in range(modes):
            upto = state[m]
            for reach in (1, 2, 4):
                moved = pltpu.roll(upto, reach, 0) * jnp.exp(rate[m] * (-float(span * reach)))
                upto = upto + jnp.where(sub >= reach, moved, 0.0)
            carry[m, :, lanes] = jnp.where(sub >= 1, pltpu.roll(upto, 1, 0), 0.0)
            ends[pl.ds(m, 1), lanes] = upto[SUBS - 1 :, :]


def back_kernel(queries, local, carry, entry, rates, residues, w_out, kept, sent, mixed):
    me = lax.axis_index("ch")
    rows, width = queries.shape
    span = rows // SUBS
    modes = rates.shape[0]
    sub = lax.broadcasted_iota(jnp.int32, (SUBS, LANES), 0).astype(F32)
    for lane in range(0, width, LANES):
        lanes = pl.ds(lane, LANES)
        rate = [row(rates, m, lanes) for m in range(modes)]
        decay = [jnp.exp(-r) for r in rate]
        state = []
        for m in range(modes):
            weight = row(residues, m, lanes) * jnp.sqrt(rate[m]) * decay[m]
            entering = carry[m, :, lanes] + jnp.exp(rate[m] * sub * (-float(span))) * row(entry, m, lanes)
            state.append(weight * entering)

        def step(index, held):
            at = pl.ds(pl.multiple_of(index * SUBS, SUBS), SUBS)
            terms = list(held) + [local[at, lanes]]
            while len(terms) > 1:
                terms = [sum(terms[i : i + 2][1:], terms[i]) for i in range(0, len(terms), 2)]
            mixed[lane // LANES, pl.ds(index, SUBS, stride=span), :] = queries[at, lanes] * terms[0]
            return [decay[m] * held[m] for m in range(modes)]

        lax.fori_loop(0, span, step, state, unroll=4)
    mixed_in = jnp.concatenate([mixed[tile] for tile in range(width // LANES)], axis=1).astype(BF16)
    for order in range(4):
        start = pl.multiple_of(jnp.bitwise_xor(me, order) * width, width)
        share = jnp.dot(mixed_in, w_out[:, pl.ds(start, width)], preferred_element_type=F32)
        if order % 2 == 0:
            kept[order // 2] = share
        else:
            sent[order // 2] = share.astype(BF16)


def halo_tokens(tokens):
    blocks, chs = lax.axis_size("seq"), lax.axis_size("ch")
    tail = tokens[tokens.shape[0] - HALO :]
    pair = jnp.stack([tail, ch_swap(tail, 1)])
    moves = [
        (chs * block + c, chs * (block + 1) + (c if c % 2 == 0 else c ^ 2))
        for block in range(blocks - 1)
        for c in range(chs)
    ]
    mine = lax.ppermute(pair, ("seq", "ch"), moves)
    other = ch_swap(mine, 1)
    even = lax.axis_index("ch") % 2 == 0
    low = jnp.where(even, mine, other[::-1])
    high = jnp.where(even, other[::-1], mine)
    return jnp.concatenate([low, high], axis=0)


def scan_blocks(ends, rates, rows):
    block = lax.axis_index("seq")
    rounds = lax.axis_size("seq").bit_length() - 1
    total = ends
    entry = jnp.zeros_like(ends)
    for level in range(rounds):
        other = seq_swap(total, SCAN_MASKS[level])
        upper = jnp.bitwise_and(jnp.right_shift(block, level), 1) == 1
        ahead = jnp.remainder(block, 1 << level).astype(F32) * float(rows)
        across = jnp.exp(-rates * float(rows << level))
        entry = jnp.where(upper, entry + jnp.exp(-rates * ahead) * other, entry)
        total = jnp.where(upper, across * other + total, across * total + other)
    return entry


def body(tokens, norm_gain, w_in, short_filter, rates, residues, skip_gain, w_out):
    rows, width = tokens.shape
    slab = w_in.shape[0]
    channels = w_in.shape[2]
    modes = rates.shape[0]
    taps = short_filter.reshape(-1, channels)
    far = ch_swap(tokens, 2)
    halo = halo_tokens(tokens)
    side = ch_swap(tokens, 1)
    side_far = ch_swap(far, 1)
    queries, local, carry, ends = pl.pallas_call(
        front_kernel,
        out_shape=(
            jax.ShapeDtypeStruct((rows, channels), F32),
            jax.ShapeDtypeStruct((rows, channels), F32),
            jax.ShapeDtypeStruct((modes, SUBS, channels), F32),
            jax.ShapeDtypeStruct((modes, channels), F32),
        ),
        in_specs=vmem_specs(11),
        out_specs=tuple(vmem_specs(4)),
        scratch_shapes=[pltpu.VMEM((3 * channels // LANES, rows + HALO, LANES), F32)],
        compiler_params=pltpu.CompilerParams(vmem_limit_bytes=VMEM_LIMIT),
        name="front",
    )(
        tokens, far, side, side_far, halo, norm_gain.reshape(-1, width), w_in.reshape(slab, 3 * channels),
        taps, rates, residues, skip_gain.reshape(1, channels),
    )
    entry = scan_blocks(ends, rates, rows)
    kept, sent = pl.pallas_call(
        back_kernel,
        out_shape=(
            jax.ShapeDtypeStruct((2, rows, width), F32),
            jax.ShapeDtypeStruct((2, rows, width), BF16),
        ),
        in_specs=vmem_specs(7),
        out_specs=tuple(vmem_specs(2)),
        scratch_shapes=[pltpu.VMEM((channels // LANES, rows, LANES), F32)],
        compiler_params=pltpu.CompilerParams(vmem_limit_bytes=VMEM_LIMIT),
        name="back",
    )(queries, local, carry, entry, rates, residues, w_out)
    both = kept + ch_swap(sent, 1).astype(F32)
    away = ch_swap(both[1].astype(BF16), 2)
    return (both[0] + away.astype(F32)).astype(BF16)


def solution(mesh):
    return jax.shard_map(
        body,
        mesh=mesh,
        in_specs=(
            P("seq", "ch"),
            P(),
            P(None, None, "ch"),
            P(None, None, "ch"),
            P(None, "ch"),
            P(None, "ch"),
            P("ch"),
            P("ch", None),
        ),
        out_specs=P("seq", "ch"),
        check_vma=False,
    )
```

```python
import jax
import jax.numpy as jnp
from jax import lax
from jax.experimental import pallas as pl
from jax.experimental.pallas import tpu as pltpu
from jax.sharding import PartitionSpec as P

EPSILON = 1e-06
F32 = jnp.float32
BF16 = jnp.bfloat16
LANES = 128
SUBS = 8
HALO = 16
STAGE_VMEM = 2 * 1024 * 1024
FRONT_VMEM = 16 * 1024 * 1024
SCAN_VMEM = 8 * 1024 * 1024
BACK_VMEM = 12 * 1024 * 1024

SCAN_MASKS = (1, 3, 4, 8, 24, 32)


def ch_swap(array, mask):
    return lax.ppermute(array, "ch", [(i, i ^ mask) for i in range(lax.axis_size("ch"))])


def seq_swap(array, mask):
    return lax.ppermute(array, "seq", [(i, i ^ mask) for i in range(lax.axis_size("seq"))])


def vmem_specs(count):
    return [pl.BlockSpec(memory_space=pltpu.VMEM)] * count


def row(ref, index, lanes):
    return jnp.broadcast_to(ref[pl.ds(index, 1), lanes], (SUBS, LANES))


def tree_sum(terms):
    while len(terms) > 1:
        terms = [sum(terms[i : i + 2][1:], terms[i]) for i in range(0, len(terms), 2)]
    return terms[0]


def stage_kernel(own, w_in, taps, rates, gain, own_v, w_in_v, taps_v, rates_v, gain_v, sems):
    pairs = ((own, own_v), (w_in, w_in_v), (taps, taps_v), (rates, rates_v), (gain, gain_v))
    copies = [pltpu.make_async_copy(src, dst, sems.at[i]) for i, (src, dst) in enumerate(pairs)]
    for copy in copies:
        copy.start()
    for copy in copies:
        copy.wait()


def front_kernel(
    own, far, side, side_far, gain, w_in, taps, rates,
    queries, gated, message, projected,
):
    me = lax.axis_index("ch")
    rows, width = own.shape
    span = rows // SUBS
    modes = rates.shape[0]
    tiles = width // LANES
    square = jnp.zeros((rows, LANES), F32)
    blocks = (own, side, far, side_far)
    for block in blocks:
        for lane in range(0, width, LANES):
            piece = block[:, lane : lane + LANES].astype(F32)
            square = square + piece * piece
    scale = lax.rsqrt(jnp.sum(square, axis=1, keepdims=True) * (1.0 / (4 * width)) + EPSILON)
    normed = []
    for order, block in enumerate(blocks):
        part = jnp.bitwise_xor(me, order)
        pieces = [
            block[:, tile * LANES : (tile + 1) * LANES].astype(F32) * scale * gain[pl.ds(part * tiles + tile, 1), :]
            for tile in range(tiles)
        ]
        normed.append(jnp.concatenate(pieces, axis=1).astype(BF16))
    for group in range(3):
        total = jnp.zeros((rows, width), F32)
        for order in range(4):
            start = pl.multiple_of(jnp.bitwise_xor(me, order) * width, width)
            total = total + jnp.dot(
                normed[order], w_in[group, pl.ds(start, width), :], preferred_element_type=F32
            )
        total = total.astype(BF16).astype(F32)
        for tile in range(tiles):
            projected[group * tiles + tile, :HALO] = jnp.zeros((HALO, LANES), F32)
            projected[group * tiles + tile, HALO:] = total[:, tile * LANES : (tile + 1) * LANES]

    sub = lax.broadcasted_iota(jnp.int32, (SUBS, LANES), 0)
    message[...] = jnp.zeros_like(message)
    for tile in range(tiles):
        lanes = pl.ds(tile * LANES, LANES)
        rate = [row(rates, m, lanes) for m in range(modes)]
        decay = [jnp.exp(-r) for r in rate]
        tap = [[jnp.broadcast_to(taps[s, pl.ds(g, 1), lanes], (SUBS, LANES)) for s in range(3)] for g in range(3)]

        def read(start, group):
            return projected[group * tiles + tile, pl.ds(start, SUBS, stride=span), :]

        def step(index, held):
            before, state = held
            now = [read(HALO + index, g) for g in range(3)]
            filtered = [
                tap[g][0] * now[g] + tap[g][1] * before[0][g] + tap[g][2] * before[1][g] for g in range(3)
            ]
            product = filtered[1] * filtered[2]
            at = pl.ds(pl.multiple_of(index * SUBS, SUBS), SUBS)
            queries[at, lanes] = filtered[0]
            gated[at, lanes] = product
            return ((now, before[0]), [decay[m] * state[m] + product for m in range(modes)])

        first = ([read(HALO - 1, g) for g in range(3)], [read(HALO - 2, g) for g in range(3)])
        zeros = [jnp.zeros((SUBS, LANES), F32)] * modes
        _, state = lax.fori_loop(0, span, step, (first, zeros), unroll=8)
        for m in range(modes):
            upto = state[m] * jnp.exp(rate[m] * (float(span) * (sub - (SUBS - 1)).astype(F32)))
            message[pl.ds(m, 1), lanes] = jnp.sum(upto, axis=0, keepdims=True)
        for group in range(3):
            t = [taps[s, pl.ds(group, 1), lanes] for s in range(3)]
            p = [projected[group * tiles + tile, pl.ds(HALO + i, 1), :] for i in (0, 1, rows - 2, rows - 1)]
            if group > 0:
                message[pl.ds(modes + 2 * group - 2, 1), lanes] = t[0] * p[0]
                message[pl.ds(modes + 2 * group - 1, 1), lanes] = t[0] * p[1] + t[1] * p[0]
            to = modes + SUBS + 2 * ((group - 1) % 3)
            message[pl.ds(to, 1), lanes] = t[1] * p[3] + t[2] * p[2]
            message[pl.ds(to + 1, 1), lanes] = t[2] * p[3]


def scan_kernel(gated, rates, residues, skip, local, carry):
    rows, width = gated.shape
    span = rows // SUBS
    modes = rates.shape[0]
    sub = lax.broadcasted_iota(jnp.int32, (SUBS, LANES), 0)
    for lane in range(0, width, LANES):
        lanes = pl.ds(lane, LANES)
        rate = [row(rates, m, lanes) for m in range(modes)]
        decay = [jnp.exp(-r) for r in rate]
        weight = [row(residues, m, lanes) * jnp.sqrt(rate[m]) for m in range(modes)]
        skip_row = row(skip, 0, lanes)

        def step(index, state):
            at = pl.ds(pl.multiple_of(index * SUBS, SUBS), SUBS)
            product = gated[at, lanes]
            state = [decay[m] * state[m] + product for m in range(modes)]
            local[at, lanes] = tree_sum([weight[m] * state[m] for m in range(modes)] + [skip_row * product])
            return state

        state = lax.fori_loop(0, span, step, [jnp.zeros((SUBS, LANES), F32)] * modes, unroll=8)
        for m in range(modes):
            upto = state[m]
            for reach in (1, 2, 4):
                moved = pltpu.roll(upto, reach, 0) * jnp.exp(rate[m] * (-float(span * reach)))
                upto = upto + jnp.where(sub >= reach, moved, 0.0)
            carry[m, :, lanes] = jnp.where(sub >= 1, pltpu.roll(upto, 1, 0), 0.0)


def back_kernel(
    queries, local, carry, entry, fix, rates, residues, skip, w_out, kept, sent, mixed
):
    me = lax.axis_index("ch")
    rows, width = queries.shape
    span = rows // SUBS
    modes = rates.shape[0]
    sub = lax.broadcasted_iota(jnp.int32, (SUBS, LANES), 0)
    for lane in range(0, width, LANES):
        lanes = pl.ds(lane, LANES)
        rate = [row(rates, m, lanes) for m in range(modes)]
        decay = [jnp.exp(-r) for r in rate]
        state, lead = [], []
        for m in range(modes):
            weight = row(residues, m, lanes) * jnp.sqrt(rate[m])
            entering = carry[m, :, lanes]
            entering = entering + jnp.exp(rate[m] * sub.astype(F32) * (-float(span))) * row(entry, m, lanes)
            state.append(weight * decay[m] * entering)
            lead.append(weight * jnp.exp(rate[m]))

        def token(index, held, more_local=None, more_query=None):
            at = pl.ds(pl.multiple_of(index * SUBS, SUBS), SUBS)
            value, query = local[at, lanes], queries[at, lanes]
            if more_local is not None:
                value = value + jnp.where(sub == 0, more_local, 0.0)
                query = query + jnp.where(sub == 0, more_query, 0.0)
            mixed[lane // LANES, pl.ds(index, SUBS, stride=span), :] = query * tree_sum(list(held) + [value])
            return [decay[m] * held[m] for m in range(modes)]

        skip_row = row(skip, 0, lanes)
        more = [row(fix, i, lanes) for i in range(4)]
        state = token(0, state, skip_row * more[0] - tree_sum(lead) * more[1], more[2])
        state = token(1, state, skip_row * more[1], more[3])
        lax.fori_loop(2, span, token, state, unroll=2)
    mixed_in = jnp.concatenate([mixed[tile] for tile in range(width // LANES)], axis=1).astype(BF16)
    for order in range(4):
        start = pl.multiple_of(jnp.bitwise_xor(me, order) * width, width)
        share = jnp.dot(mixed_in, w_out[:, pl.ds(start, width)], preferred_element_type=F32)
        if order % 2 == 0:
            kept[order // 2] = share
        else:
            sent[order // 2] = share.astype(BF16)


def scan_blocks(message, rates, rows):
    block = lax.axis_index("seq")
    rounds = lax.axis_size("seq").bit_length() - 1
    modes = rates.shape[0]
    back_one, back_two = jnp.exp(rates), jnp.exp(2.0 * rates)
    entry = jnp.zeros_like(rates)
    fix = jnp.zeros((4,) + rates.shape[1:], F32)
    for level in range(rounds):
        other = seq_swap(message, SCAN_MASKS[level])
        upper = jnp.bitwise_and(jnp.right_shift(block, level), 1) == 1
        ahead = jnp.bitwise_and(block, (1 << level) - 1)
        decay_ahead = jnp.exp(-rates * (ahead.astype(F32) * float(rows)))
        across = jnp.exp(-rates * float(rows << level))
        first = jnp.where(upper, other, message)
        second = jnp.where(upper, message, other)
        start = second[modes : modes + SUBS]
        end = first[modes + SUBS :]
        added = start[0:2] * end[2:4] + end[0:2] * (start[2:4] + end[2:4])
        joined = first[:modes] + back_one * added[0:1] + back_two * added[1:2]
        entry = jnp.where(upper, entry + decay_ahead * joined, entry)
        fix = jnp.where(
            jnp.logical_and(upper, ahead == 0), jnp.concatenate([added, end[4:6]], axis=0), fix
        )
        message = jnp.concatenate(
            [across * joined + second[:modes], first[modes : modes + SUBS], second[modes + SUBS :]], axis=0
        )
    return entry, fix


def body(tokens, norm_gain, w_in, short_filter, rates, residues, skip_gain, w_out):
    rows, width = tokens.shape
    channels = w_in.shape[2]
    modes = rates.shape[0]
    skip = skip_gain.reshape(1, channels)
    far = ch_swap(tokens, 2)
    side = ch_swap(tokens, 1)
    weights = jnp.transpose(w_in, (1, 0, 2))
    gains = norm_gain.reshape(-1, LANES)
    staged = (tokens, weights, short_filter, rates, gains)
    staged = pl.pallas_call(
        stage_kernel,
        out_shape=tuple(jax.ShapeDtypeStruct(a.shape, a.dtype) for a in staged),
        in_specs=[pl.BlockSpec(memory_space=pl.ANY)] * len(staged),
        out_specs=tuple(vmem_specs(len(staged))),
        scratch_shapes=[pltpu.SemaphoreType.DMA((len(staged),))],
        compiler_params=pltpu.CompilerParams(vmem_limit_bytes=STAGE_VMEM),
        name="stage",
    )(*staged)
    far, staged = lax.optimization_barrier((far, staged))
    side_far = ch_swap(far, 1)
    own_v, w_in_v, taps_v, rates_v, gain_v = staged
    queries, gated, message = pl.pallas_call(
        front_kernel,
        out_shape=(
            jax.ShapeDtypeStruct((rows, channels), F32),
            jax.ShapeDtypeStruct((rows, channels), F32),
            jax.ShapeDtypeStruct((modes + 2 * SUBS, channels), F32),
        ),
        in_specs=vmem_specs(8),
        out_specs=tuple(vmem_specs(3)),
        scratch_shapes=[pltpu.VMEM((3 * channels // LANES, rows + HALO, LANES), F32)],
        compiler_params=pltpu.CompilerParams(vmem_limit_bytes=FRONT_VMEM),
        cost_estimate=pl.CostEstimate(flops=900_000_000, bytes_accessed=4_000_000, transcendentals=0),
        name="front",
    )(
        own_v, far, side, side_far, gain_v, w_in_v, taps_v, rates_v,
    )
    local, carry = pl.pallas_call(
        scan_kernel,
        out_shape=(
            jax.ShapeDtypeStruct((rows, channels), F32),
            jax.ShapeDtypeStruct((modes, SUBS, channels), F32),
        ),
        in_specs=vmem_specs(4),
        out_specs=tuple(vmem_specs(2)),
        compiler_params=pltpu.CompilerParams(vmem_limit_bytes=SCAN_VMEM),
        cost_estimate=pl.CostEstimate(flops=2_000_000_000, bytes_accessed=1_000_000, transcendentals=0),
        name="scan",
    )(gated, rates_v, residues, skip)
    entry, fix = scan_blocks(message, rates_v, rows)
    kept, sent = pl.pallas_call(
        back_kernel,
        out_shape=(
            jax.ShapeDtypeStruct((2, rows, width), F32),
            jax.ShapeDtypeStruct((2, rows, width), BF16),
        ),
        in_specs=vmem_specs(9),
        out_specs=tuple(vmem_specs(2)),
        scratch_shapes=[pltpu.VMEM((channels // LANES, rows, LANES), F32)],
        compiler_params=pltpu.CompilerParams(vmem_limit_bytes=BACK_VMEM),
        cost_estimate=pl.CostEstimate(flops=900_000_000, bytes_accessed=4_000_000, transcendentals=0),
        name="back",
    )(queries, local, carry, entry, fix, rates_v, residues, skip, w_out)
    both = kept + ch_swap(sent, 1).astype(F32)
    away = ch_swap(both[1].astype(BF16), 2)
    return (both[0] + away.astype(F32)).astype(BF16)


def solution(mesh):
    return jax.shard_map(
        body,
        mesh=mesh,
        in_specs=(
            P("seq", "ch"),
            P(),
            P(None, None, "ch"),
            P(None, None, "ch"),
            P(None, "ch"),
            P(None, "ch"),
            P("ch"),
            P("ch", None),
        ),
        out_specs=P("seq", "ch"),
        check_vma=False,
    )
```

```python
import jax
import jax.numpy as jnp
from jax import lax
from jax.experimental import pallas as pl
from jax.experimental.pallas import tpu as pltpu
from jax.sharding import PartitionSpec as P

EPSILON = 1e-06
F32 = jnp.float32
BF16 = jnp.bfloat16
LANES = 128
SUBS = 8
HALO = 16
STAGE_VMEM = 2 * 1024 * 1024
FRONT_VMEM = 16 * 1024 * 1024
SCAN_VMEM = 8 * 1024 * 1024
BACK_VMEM = 12 * 1024 * 1024

SCAN_FIRST = ((1,), (3,))
SCAN_LATER = ((4, 8, 12), (24,), (32,))


def ch_swap(array, mask):
    return lax.ppermute(array, "ch", [(i, i ^ mask) for i in range(lax.axis_size("ch"))])


def seq_swap(array, mask):
    return lax.ppermute(array, "seq", [(i, i ^ mask) for i in range(lax.axis_size("seq"))])


def vmem_specs(count):
    return [pl.BlockSpec(memory_space=pltpu.VMEM)] * count


def row(ref, index, lanes):
    return jnp.broadcast_to(ref[pl.ds(index, 1), lanes], (SUBS, LANES))


def tree_sum(terms):
    while len(terms) > 1:
        terms = [sum(terms[i : i + 2][1:], terms[i]) for i in range(0, len(terms), 2)]
    return terms[0]


def stage_kernel(own, w_in, taps, rates, gain, own_v, w_in_v, taps_v, rates_v, gain_v, sems):
    pairs = ((own, own_v), (w_in, w_in_v), (taps, taps_v), (rates, rates_v), (gain, gain_v))
    copies = [pltpu.make_async_copy(src, dst, sems.at[i]) for i, (src, dst) in enumerate(pairs)]
    for copy in copies:
        copy.start()
    for copy in copies:
        copy.wait()


def front_kernel(
    own, far, side, side_far, gain, w_in, taps, rates,
    queries, gated, message, projected,
):
    me = lax.axis_index("ch")
    rows, width = own.shape
    span = rows // SUBS
    modes = rates.shape[0]
    tiles = width // LANES
    square = jnp.zeros((rows, LANES), F32)
    blocks = (own, side, far, side_far)
    for block in blocks:
        for lane in range(0, width, LANES):
            piece = block[:, lane : lane + LANES].astype(F32)
            square = square + piece * piece
    scale = lax.rsqrt(jnp.sum(square, axis=1, keepdims=True) * (1.0 / (4 * width)) + EPSILON)
    normed = []
    for order, block in enumerate(blocks):
        part = jnp.bitwise_xor(me, order)
        pieces = [
            block[:, tile * LANES : (tile + 1) * LANES].astype(F32) * scale * gain[pl.ds(part * tiles + tile, 1), :]
            for tile in range(tiles)
        ]
        normed.append(jnp.concatenate(pieces, axis=1).astype(BF16))
    for group in range(3):
        total = jnp.zeros((rows, width), F32)
        for order in range(4):
            start = pl.multiple_of(jnp.bitwise_xor(me, order) * width, width)
            total = total + jnp.dot(
                normed[order], w_in[group, pl.ds(start, width), :], preferred_element_type=F32
            )
        total = total.astype(BF16).astype(F32)
        for tile in range(tiles):
            projected[group * tiles + tile, :HALO] = jnp.zeros((HALO, LANES), F32)
            projected[group * tiles + tile, HALO:] = total[:, tile * LANES : (tile + 1) * LANES]

    sub = lax.broadcasted_iota(jnp.int32, (SUBS, LANES), 0)
    message[...] = jnp.zeros_like(message)
    for tile in range(tiles):
        lanes = pl.ds(tile * LANES, LANES)
        rate = [row(rates, m, lanes) for m in range(modes)]
        decay = [jnp.exp(-r) for r in rate]
        tap = [[jnp.broadcast_to(taps[s, pl.ds(g, 1), lanes], (SUBS, LANES)) for s in range(3)] for g in range(3)]

        def read(start, group):
            return projected[group * tiles + tile, pl.ds(start, SUBS, stride=span), :]

        def step(index, held):
            before, state = held
            now = [read(HALO + index, g) for g in range(3)]
            filtered = [
                tap[g][0] * now[g] + tap[g][1] * before[0][g] + tap[g][2] * before[1][g] for g in range(3)
            ]
            product = filtered[1] * filtered[2]
            at = pl.ds(pl.multiple_of(index * SUBS, SUBS), SUBS)
            queries[at, lanes] = filtered[0]
            gated[at, lanes] = product
            return ((now, before[0]), [decay[m] * state[m] + product for m in range(modes)])

        first = ([read(HALO - 1, g) for g in range(3)], [read(HALO - 2, g) for g in range(3)])
        zeros = [jnp.zeros((SUBS, LANES), F32)] * modes
        _, state = lax.fori_loop(0, span, step, (first, zeros), unroll=8)
        for m in range(modes):
            upto = state[m] * jnp.exp(rate[m] * (float(span) * (sub - (SUBS - 1)).astype(F32)))
            message[pl.ds(m, 1), lanes] = jnp.sum(upto, axis=0, keepdims=True)
        for group in range(3):
            t = [taps[s, pl.ds(group, 1), lanes] for s in range(3)]
            p = [projected[group * tiles + tile, pl.ds(HALO + i, 1), :] for i in (0, 1, rows - 2, rows - 1)]
            if group > 0:
                message[pl.ds(modes + 2 * group - 2, 1), lanes] = t[0] * p[0]
                message[pl.ds(modes + 2 * group - 1, 1), lanes] = t[0] * p[1] + t[1] * p[0]
            to = modes + SUBS + 2 * ((group - 1) % 3)
            message[pl.ds(to, 1), lanes] = t[1] * p[3] + t[2] * p[2]
            message[pl.ds(to + 1, 1), lanes] = t[2] * p[3]


def scan_kernel(queries, gated, rates, residues, skip, w_out, local, pack):
    rows, width = gated.shape
    other = 1 - jnp.right_shift(lax.axis_index("ch"), 1)
    for column in range(2):
        start = pl.multiple_of((2 * other + column) * width, width)
        pack[2, column * width : (column + 1) * width, :] = w_out[:, pl.ds(start, width)]
    span = rows // SUBS
    modes = rates.shape[0]
    sub = lax.broadcasted_iota(jnp.int32, (SUBS, LANES), 0)
    for lane in range(0, width, LANES):
        lanes = pl.ds(lane, LANES)
        rate = [row(rates, m, lanes) for m in range(modes)]
        decay = [jnp.exp(-r) for r in rate]
        weight = [row(residues, m, lanes) * jnp.sqrt(rate[m]) for m in range(modes)]
        skip_row = row(skip, 0, lanes)

        def step(index, state):
            at = pl.ds(pl.multiple_of(index * SUBS, SUBS), SUBS)
            product = gated[at, lanes]
            state = [decay[m] * state[m] + product for m in range(modes)]
            local[at, lanes] = tree_sum([weight[m] * state[m] for m in range(modes)] + [skip_row * product])
            return state

        state = lax.fori_loop(0, span, step, [jnp.zeros((SUBS, LANES), F32)] * modes, unroll=8)
        brought = []
        for m in range(modes):
            upto = state[m]
            for reach in (1, 2, 4):
                moved = pltpu.roll(upto, reach, 0) * jnp.exp(rate[m] * (-float(span * reach)))
                upto = upto + jnp.where(sub >= reach, moved, 0.0)
            brought.append(weight[m] * decay[m] * jnp.where(sub >= 1, pltpu.roll(upto, 1, 0), 0.0))

        def add(index, held):
            both = []
            for half in range(2):
                at = pl.ds(pl.multiple_of((2 * index + half) * SUBS, SUBS), SUBS)
                both.append(tree_sum(list(held) + [local[at, lanes]]))
                local[at, lanes] = both[-1]
                held = [decay[m] * held[m] for m in range(modes)]
            at = pl.ds(pl.multiple_of(index * 2 * SUBS, 2 * SUBS), 2 * SUBS)
            pack[0, at, lanes] = queries[at, lanes].astype(BF16)
            pack[1, at, lanes] = jnp.concatenate(both, axis=0).astype(BF16)
            return held

        lax.fori_loop(0, span // 2, add, brought, unroll=2)


def mix(read, entry, mixed):
    tiles, rows = mixed.shape[:2]
    span = rows // SUBS
    modes = (entry.shape[0] - SUBS) // 2
    sub = lax.broadcasted_iota(jnp.int32, (SUBS, LANES), 0)
    for tile in range(tiles):
        lanes = pl.ds(tile * LANES, LANES)
        rate = [row(entry, modes + SUBS + m, lanes) for m in range(modes)]
        decay = [jnp.exp(-r) for r in rate]
        state = [jnp.exp(rate[m] * sub.astype(F32) * (-float(span))) * row(entry, m, lanes) for m in range(modes)]

        def pair(index, held, more=None):
            at = pl.ds(pl.multiple_of(index * 2 * SUBS, 2 * SUBS), 2 * SUBS)
            query, value = read(at, lanes)
            for half in range(2):
                v, q = value[half * SUBS : (half + 1) * SUBS], query[half * SUBS : (half + 1) * SUBS]
                if more is not None:
                    v = v + jnp.where(sub == 0, more[half], 0.0)
                    q = q + jnp.where(sub == 0, more[2 + half], 0.0)
                token = 2 * index + half
                mixed[tile, pl.ds(token, SUBS, stride=span), :] = q * tree_sum(list(held) + [v])
                held = [decay[m] * held[m] for m in range(modes)]
            return held

        state = pair(0, state, [row(entry, modes + i, lanes) for i in range(4)])
        lax.fori_loop(1, span // 2, pair, state, unroll=2)
    return jnp.concatenate([mixed[tile] for tile in range(tiles)], axis=1).astype(BF16)


def near_kernel(queries, local, entry, w_out, share, mixed):
    me = lax.axis_index("ch")
    chip, core = jnp.right_shift(me, 1), jnp.bitwise_and(me, 1)
    width = queries.shape[1]
    part = mix(lambda at, lanes: (queries[at, lanes], local[at, lanes]), entry, mixed)
    for slot, column in enumerate((1 - core, core)):
        start = pl.multiple_of((2 * chip + column) * width, width)
        share[slot] = jnp.dot(part, w_out[:, pl.ds(start, width)], preferred_element_type=F32)


def far_kernel(pack, entry, share, kept, sent, mixed):
    core = jnp.bitwise_and(lax.axis_index("ch"), 1)
    width = pack.shape[2]
    part = mix(lambda at, lanes: (pack[0, at, lanes].astype(F32), pack[1, at, lanes].astype(F32)), entry, mixed)
    for slot, (target, column) in enumerate(((sent, 1 - core), (kept, core))):
        start = pl.multiple_of(column * width, width)
        total = share[slot] + jnp.dot(part, pack[2, pl.ds(start, width), :], preferred_element_type=F32)
        target[...] = total.astype(target.dtype)


def join(first, second, rates, rows):
    modes = rates.shape[0]
    start = second[modes : modes + SUBS]
    end = first[modes + SUBS :]
    added = start[0:2] * end[2:4] + end[0:2] * (start[2:4] + end[2:4])
    entering = first[:modes] + jnp.exp(rates) * added[0:1] + jnp.exp(2.0 * rates) * added[1:2]
    state = jnp.exp(-rates * float(rows)) * entering + second[:modes]
    both = jnp.concatenate([state, first[modes : modes + SUBS], second[modes + SUBS :]], axis=0)
    return both, entering, jnp.concatenate([added, end[4:6]], axis=0)


def scan_blocks(held, rates, rows, steps, level):
    block = lax.axis_index("seq")
    rounds = lax.axis_size("seq").bit_length() - 1
    message, entry, fix = held

    def place(level):
        upper = jnp.bitwise_and(jnp.right_shift(block, level), 1) == 1
        ahead = jnp.bitwise_and(block, (1 << level) - 1)
        return upper, ahead

    def ordered(upper, mine, other):
        return jnp.where(upper, other, mine), jnp.where(upper, mine, other)

    def enter(level, entry, fix, entering, added):
        upper, ahead = place(level)
        decay = jnp.exp(-rates * (ahead.astype(F32) * float(rows)))
        entry = jnp.where(upper, entry + decay * entering, entry)
        return entry, jnp.where(jnp.logical_and(upper, ahead == 0), added, fix)

    for masks in steps:
        if level >= rounds:
            break
        others = [seq_swap(message, mask) for mask in masks]
        upper, _ = place(level)
        message, entering, added = join(*ordered(upper, message, others[0]), rates, rows << level)
        entry, fix = enter(level, entry, fix, entering, added)
        if len(masks) == 3:
            pair, _, _ = join(*ordered(upper, others[1], others[2]), rates, rows << level)
            upper, _ = place(level + 1)
            message, entering, added = join(*ordered(upper, message, pair), rates, rows << (level + 1))
            entry, fix = enter(level + 1, entry, fix, entering, added)
        level += 1 if len(masks) == 1 else 2
    return message, entry, fix


def body(tokens, norm_gain, w_in, short_filter, rates, residues, skip_gain, w_out):
    rows, width = tokens.shape
    channels = w_in.shape[2]
    modes = rates.shape[0]
    skip = skip_gain.reshape(1, channels)
    far = ch_swap(tokens, 2)
    side = ch_swap(tokens, 1)
    weights = jnp.transpose(w_in, (1, 0, 2))
    gains = norm_gain.reshape(-1, LANES)
    staged = (tokens, weights, short_filter, rates, gains)
    staged = pl.pallas_call(
        stage_kernel,
        out_shape=tuple(jax.ShapeDtypeStruct(a.shape, a.dtype) for a in staged),
        in_specs=[pl.BlockSpec(memory_space=pl.ANY)] * len(staged),
        out_specs=tuple(vmem_specs(len(staged))),
        scratch_shapes=[pltpu.SemaphoreType.DMA((len(staged),))],
        compiler_params=pltpu.CompilerParams(vmem_limit_bytes=STAGE_VMEM),
        name="stage",
    )(*staged)
    far, staged = lax.optimization_barrier((far, staged))
    side_far = ch_swap(far, 1)
    own_v, w_in_v, taps_v, rates_v, gain_v = staged
    queries, gated, message = pl.pallas_call(
        front_kernel,
        out_shape=(
            jax.ShapeDtypeStruct((rows, channels), F32),
            jax.ShapeDtypeStruct((rows, channels), F32),
            jax.ShapeDtypeStruct((modes + 2 * SUBS, channels), F32),
        ),
        in_specs=vmem_specs(8),
        out_specs=tuple(vmem_specs(3)),
        scratch_shapes=[pltpu.VMEM((3 * channels // LANES, rows + HALO, LANES), F32)],
        compiler_params=pltpu.CompilerParams(vmem_limit_bytes=FRONT_VMEM),
        cost_estimate=pl.CostEstimate(flops=900_000_000, bytes_accessed=4_000_000, transcendentals=0),
        name="front",
    )(own_v, far, side, side_far, gain_v, w_in_v, taps_v, rates_v)
    local, pack = pl.pallas_call(
        scan_kernel,
        out_shape=(
            jax.ShapeDtypeStruct((rows, channels), F32),
            jax.ShapeDtypeStruct((3, rows, channels), BF16),
        ),
        in_specs=vmem_specs(6),
        out_specs=tuple(vmem_specs(2)),
        compiler_params=pltpu.CompilerParams(vmem_limit_bytes=SCAN_VMEM),
        cost_estimate=pl.CostEstimate(flops=2_000_000_000, bytes_accessed=1_000_000, transcendentals=0),
        name="scan",
    )(queries, gated, rates_v, residues, skip, w_out)
    held = (message, jnp.zeros_like(rates_v), jnp.zeros((4, channels), F32))
    held = scan_blocks(held, rates_v, rows, SCAN_FIRST[:1], 0)
    held, local, pack = lax.optimization_barrier((held, local, pack))
    pack_far = ch_swap(pack, 2)
    held = scan_blocks(held, rates_v, rows, SCAN_FIRST[1:], 1)
    once = jnp.minimum(lax.axis_index("seq") + 1, 1)
    held = lax.fori_loop(0, once, lambda _, now: scan_blocks(now, rates_v, rows, SCAN_LATER, len(SCAN_FIRST)), held)
    (_, entry, fix), pack_far = lax.optimization_barrier((held, pack_far))
    weight = residues * jnp.sqrt(rates_v)
    lead = jnp.sum(weight * jnp.exp(rates_v), axis=0, keepdims=True)
    entry = jnp.concatenate(
        [
            weight * jnp.exp(-rates_v) * entry,
            skip * fix[0:1] - lead * fix[1:2],
            skip * fix[1:2],
            fix[2:4],
            jnp.zeros_like(fix),
            rates_v,
        ],
        axis=0,
    )
    entry_far = ch_swap(entry, 2)
    share = pl.pallas_call(
        near_kernel,
        out_shape=jax.ShapeDtypeStruct((2, rows, width), F32),
        in_specs=vmem_specs(4),
        out_specs=vmem_specs(1)[0],
        scratch_shapes=[pltpu.VMEM((channels // LANES, rows, LANES), F32)],
        compiler_params=pltpu.CompilerParams(vmem_limit_bytes=BACK_VMEM),
        cost_estimate=pl.CostEstimate(flops=900_000_000, bytes_accessed=4_000_000, transcendentals=0),
        name="near",
    )(queries, local, entry, w_out)
    kept, sent = pl.pallas_call(
        far_kernel,
        out_shape=(
            jax.ShapeDtypeStruct((rows, width), F32),
            jax.ShapeDtypeStruct((rows, width), BF16),
        ),
        in_specs=vmem_specs(3),
        out_specs=tuple(vmem_specs(2)),
        scratch_shapes=[pltpu.VMEM((channels // LANES, rows, LANES), F32)],
        compiler_params=pltpu.CompilerParams(vmem_limit_bytes=BACK_VMEM),
        cost_estimate=pl.CostEstimate(flops=900_000_000, bytes_accessed=4_000_000, transcendentals=0),
        name="far",
    )(pack_far, entry_far, share)
    return (kept + ch_swap(sent, 1).astype(F32)).astype(BF16)


def solution(mesh):
    return jax.shard_map(
        body,
        mesh=mesh,
        in_specs=(
            P("seq", "ch"),
            P(),
            P(None, None, "ch"),
            P(None, None, "ch"),
            P(None, "ch"),
            P(None, "ch"),
            P("ch"),
            P("ch", None),
        ),
        out_specs=P("seq", "ch"),
        check_vma=False,
    )
```

```python
import jax
import jax.numpy as jnp
from jax import lax
from jax.experimental import pallas as pl
from jax.experimental.pallas import tpu as pltpu
from jax.sharding import PartitionSpec as P

EPSILON = 1e-06
F32 = jnp.float32
BF16 = jnp.bfloat16
LANES = 128
SUBS = 8
HALO = 16
STAGE_VMEM = 1024 * 1024
FRONT_VMEM = 8 * 1024 * 1024
SCAN_VMEM = 2 * 1024 * 1024
BACK_VMEM = 4 * 1024 * 1024

SCAN_FIRST = ((1,), (3,))
SCAN_LATER = ((4, 8, 12), (24,))
SCAN_LAST = 32

CROSSED = 0b101101


def ch_swap(array, mask):
    return lax.ppermute(array, "ch", [(i, i ^ mask) for i in range(lax.axis_size("ch"))])


def crosses(mask):
    return bin(mask & CROSSED).count("1") % 2


def crossed(block):
    bits = [jnp.right_shift(block, bit) for bit in range(CROSSED.bit_length()) if CROSSED >> bit & 1]
    total = bits[0]
    for bit in bits[1:]:
        total = jnp.bitwise_xor(total, bit)
    return jnp.bitwise_and(total, 1) == 1


def seq_swap(array, mask, chip=0):
    blocks, chs = lax.axis_size("seq"), lax.axis_size("ch")
    turn = 2 * chip ^ crosses(mask)
    pairs = [(chs * b + c, chs * (b ^ mask) + (c ^ turn)) for b in range(blocks) for c in range(chs)]
    return lax.ppermute(array, ("seq", "ch"), pairs)


def vmem_specs(count):
    return [pl.BlockSpec(memory_space=pltpu.VMEM)] * count


def row(ref, index, lanes):
    return jnp.broadcast_to(ref[pl.ds(index, 1), lanes], (SUBS, LANES))


def tree_sum(terms):
    while len(terms) > 1:
        terms = [sum(terms[i : i + 2][1:], terms[i]) for i in range(0, len(terms), 2)]
    return terms[0]


def stage_kernel(*refs):
    (own, gain), pairs, targets, sems = refs[:2], refs[2:8], refs[8:13], refs[13]
    swapped = crossed(lax.axis_index("seq"))

    def copy_all(sources):
        copies = [pltpu.make_async_copy(src, dst, sems.at[i]) for i, (src, dst) in enumerate(zip(sources, targets))]
        for copy in copies:
            copy.start()
        for copy in copies:
            copy.wait()

    @pl.when(swapped)
    def _():
        copy_all((own, gain, *pairs[1::2]))

    @pl.when(jnp.logical_not(swapped))
    def _():
        copy_all((own, gain, *pairs[::2]))


def front_kernel(
    own, far, side, side_far, gain, w_in, taps, rates,
    queries, gated, message, projected,
):
    me = lax.axis_index("ch")
    rows, width = own.shape
    span = rows // SUBS
    modes = rates.shape[0]
    tiles = width // LANES
    square = jnp.zeros((rows, LANES), F32)
    blocks = (own, side, far, side_far)
    for block in blocks:
        for lane in range(0, width, LANES):
            piece = block[:, lane : lane + LANES].astype(F32)
            square = square + piece * piece
    scale = lax.rsqrt(jnp.sum(square, axis=1, keepdims=True) * (1.0 / (4 * width)) + EPSILON)
    normed = []
    for order, block in enumerate(blocks):
        part = jnp.bitwise_xor(me, order)
        pieces = [
            block[:, tile * LANES : (tile + 1) * LANES].astype(F32) * scale * gain[pl.ds(part * tiles + tile, 1), :]
            for tile in range(tiles)
        ]
        normed.append(jnp.concatenate(pieces, axis=1).astype(BF16))
    for group in range(3):
        total = jnp.zeros((rows, width), F32)
        for order in range(4):
            start = pl.multiple_of(jnp.bitwise_xor(me, order) * width, width)
            total = total + jnp.dot(
                normed[order], w_in[group, pl.ds(start, width), :], preferred_element_type=F32
            )
        total = total.astype(BF16).astype(F32)
        for tile in range(tiles):
            projected[group * tiles + tile, :HALO] = jnp.zeros((HALO, LANES), F32)
            projected[group * tiles + tile, HALO:] = total[:, tile * LANES : (tile + 1) * LANES]

    sub = lax.broadcasted_iota(jnp.int32, (SUBS, LANES), 0)
    message[...] = jnp.zeros_like(message)
    for tile in range(tiles):
        lanes = pl.ds(tile * LANES, LANES)
        rate = [row(rates, m, lanes) for m in range(modes)]
        decay = [jnp.exp(-r) for r in rate]
        tap = [[jnp.broadcast_to(taps[s, pl.ds(g, 1), lanes], (SUBS, LANES)) for s in range(3)] for g in range(3)]

        def read(start, group):
            return projected[group * tiles + tile, pl.ds(start, SUBS, stride=span), :]

        def step(index, held):
            before, state = held
            now = [read(HALO + index, g) for g in range(3)]
            filtered = [
                tap[g][0] * now[g] + tap[g][1] * before[0][g] + tap[g][2] * before[1][g] for g in range(3)
            ]
            product = filtered[1] * filtered[2]
            at = pl.ds(pl.multiple_of(index * SUBS, SUBS), SUBS)
            queries[at, lanes] = filtered[0]
            gated[at, lanes] = product
            return ((now, before[0]), [decay[m] * state[m] + product for m in range(modes)])

        first = ([read(HALO - 1, g) for g in range(3)], [read(HALO - 2, g) for g in range(3)])
        zeros = [jnp.zeros((SUBS, LANES), F32)] * modes
        _, state = lax.fori_loop(0, span, step, (first, zeros), unroll=8)
        for m in range(modes):
            upto = state[m] * jnp.exp(rate[m] * (float(span) * (sub - (SUBS - 1)).astype(F32)))
            message[pl.ds(m, 1), lanes] = jnp.sum(upto, axis=0, keepdims=True)
        for group in range(3):
            t = [taps[s, pl.ds(group, 1), lanes] for s in range(3)]
            p = [projected[group * tiles + tile, pl.ds(HALO + i, 1), :] for i in (0, 1, rows - 2, rows - 1)]
            if group > 0:
                message[pl.ds(modes + 2 * group - 2, 1), lanes] = t[0] * p[0]
                message[pl.ds(modes + 2 * group - 1, 1), lanes] = t[0] * p[1] + t[1] * p[0]
            to = modes + SUBS + 2 * ((group - 1) % 3)
            message[pl.ds(to, 1), lanes] = t[1] * p[3] + t[2] * p[2]
            message[pl.ds(to + 1, 1), lanes] = t[2] * p[3]


def scan_kernel(
    queries, gated, rates, residues, residues_side, skip, skip_side, w_out, w_out_side, pack, extra, w_out_v, local
):
    rows, width = gated.shape
    modes = rates.shape[0]
    swapped = crossed(lax.axis_index("seq"))

    def keep(weights, direct, projection):
        extra[:modes] = weights[...]
        extra[modes:] = jnp.concatenate([direct[...], jnp.zeros((SUBS - 1, width), F32)], axis=0)
        w_out_v[...] = projection[...]

    @pl.when(swapped)
    def _():
        keep(residues_side, skip_side, w_out_side)

    @pl.when(jnp.logical_not(swapped))
    def _():
        keep(residues, skip, w_out)

    other = 1 - jnp.right_shift(lax.axis_index("ch"), 1)
    for column in range(2):
        start = pl.multiple_of((2 * other + column) * width, width)
        pack[2, column * width : (column + 1) * width, :] = w_out_v[:, pl.ds(start, width)]
    span = rows // SUBS
    sub = lax.broadcasted_iota(jnp.int32, (SUBS, LANES), 0)
    for lane in range(0, width, LANES):
        lanes = pl.ds(lane, LANES)
        rate = [row(rates, m, lanes) for m in range(modes)]
        decay = [jnp.exp(-r) for r in rate]
        weight = [row(extra, m, lanes) * jnp.sqrt(rate[m]) for m in range(modes)]
        skip_row = row(extra, modes, lanes)

        def step(index, state):
            at = pl.ds(pl.multiple_of(index * SUBS, SUBS), SUBS)
            product = gated[at, lanes]
            state = [decay[m] * state[m] + product for m in range(modes)]
            local[at, lanes] = tree_sum([weight[m] * state[m] for m in range(modes)] + [skip_row * product])
            return state

        state = lax.fori_loop(0, span, step, [jnp.zeros((SUBS, LANES), F32)] * modes, unroll=8)
        brought = []
        for m in range(modes):
            upto = state[m]
            for reach in (1, 2, 4):
                moved = pltpu.roll(upto, reach, 0) * jnp.exp(rate[m] * (-float(span * reach)))
                upto = upto + jnp.where(sub >= reach, moved, 0.0)
            brought.append(weight[m] * decay[m] * jnp.where(sub >= 1, pltpu.roll(upto, 1, 0), 0.0))

        def add(index, held):
            both = []
            for half in range(2):
                at = pl.ds(pl.multiple_of((2 * index + half) * SUBS, SUBS), SUBS)
                both.append(tree_sum(list(held) + [local[at, lanes]]))
                held = [decay[m] * held[m] for m in range(modes)]
            at = pl.ds(pl.multiple_of(index * 2 * SUBS, 2 * SUBS), 2 * SUBS)
            pack[0, at, lanes] = queries[at, lanes].astype(BF16)
            pack[1, at, lanes] = jnp.concatenate(both, axis=0).astype(BF16)
            return held

        lax.fori_loop(0, span // 2, add, brought, unroll=2)


def mix(read, mine, other, entry, mixed):
    tiles, rows = mixed.shape[:2]
    span = rows // SUBS
    modes = (mine.shape[0] - 3 * SUBS) // 3
    block, half = lax.axis_index("seq"), lax.axis_size("seq") // 2
    upper = (block >= half).astype(F32)
    first = (block == half).astype(F32)
    passed = (jnp.maximum(block - half, 0) * rows).astype(F32)
    fix, start, end = mine[modes : modes + 4], mine[modes + SUBS : modes + 2 * SUBS], other[modes + SUBS :]
    rates = mine[modes + 2 * SUBS : 2 * modes + 2 * SUBS]
    weights = mine[2 * modes + 2 * SUBS : 3 * modes + 2 * SUBS]
    skip, lead = mine[3 * modes + 2 * SUBS : 3 * modes + 2 * SUBS + 1], mine[3 * modes + 2 * SUBS + 1 : 3 * modes + 2 * SUBS + 2]
    added = start[0:2] * end[2:4] + end[0:2] * (start[2:4] + end[2:4])
    joined = other[:modes] + jnp.exp(rates) * added[0:1] + jnp.exp(2.0 * rates) * added[1:2]
    entry[:modes] = weights * (mine[:modes] + upper * jnp.exp(-rates * passed) * joined)
    added = fix[0:2] + first * added
    entry[modes : modes + 1] = skip * added[0:1] - lead * added[1:2]
    entry[modes + 1 : modes + 2] = skip * added[1:2]
    entry[modes + 2 : modes + 4] = fix[2:4] + first * end[4:6]
    sub = lax.broadcasted_iota(jnp.int32, (SUBS, LANES), 0)
    for tile in range(tiles):
        lanes = pl.ds(tile * LANES, LANES)
        rate = [row(mine, modes + 2 * SUBS + m, lanes) for m in range(modes)]
        decay = [jnp.exp(-r) for r in rate]
        state = [jnp.exp(rate[m] * sub.astype(F32) * (-float(span))) * row(entry, m, lanes) for m in range(modes)]
        more = [row(entry, modes + i, lanes) for i in range(4)]

        def pair(index, held, more=None):
            at = pl.ds(pl.multiple_of(index * 2 * SUBS, 2 * SUBS), 2 * SUBS)
            query, value = (part.astype(F32) for part in read(at, lanes))
            for half in range(2):
                v, q = value[half * SUBS : (half + 1) * SUBS], query[half * SUBS : (half + 1) * SUBS]
                if more is not None:
                    v = v + jnp.where(sub == 0, more[half], 0.0)
                    q = q + jnp.where(sub == 0, more[2 + half], 0.0)
                token = 2 * index + half
                mixed[tile, pl.ds(token, SUBS, stride=span), :] = q * tree_sum(list(held) + [v])
                held = [decay[m] * held[m] for m in range(modes)]
            return held

        state = pair(0, state, more)
        lax.fori_loop(1, span // 2, pair, state, unroll=2)
    return jnp.concatenate([mixed[tile] for tile in range(tiles)], axis=1).astype(BF16)


def near_kernel(pack, mine, other, w_out, share, entry, mixed):
    me = lax.axis_index("ch")
    chip, core = jnp.right_shift(me, 1), jnp.bitwise_and(me, 1)
    width = pack.shape[2]
    part = mix(lambda at, lanes: (pack[0, at, lanes], pack[1, at, lanes]), mine, other, entry, mixed)
    for slot, column in enumerate((1 - core, core)):
        start = pl.multiple_of((2 * chip + column) * width, width)
        share[slot] = jnp.dot(part, w_out[:, pl.ds(start, width)], preferred_element_type=F32)


def far_kernel(pack, mine, other, share, kept, sent, entry, mixed):
    core = jnp.bitwise_and(lax.axis_index("ch"), 1)
    width = pack.shape[2]
    part = mix(lambda at, lanes: (pack[0, at, lanes], pack[1, at, lanes]), mine, other, entry, mixed)
    for slot, (target, column) in enumerate(((sent, 1 - core), (kept, core))):
        start = pl.multiple_of(column * width, width)
        total = share[slot] + jnp.dot(part, pack[2, pl.ds(start, width), :], preferred_element_type=F32)
        target[...] = total.astype(target.dtype)


def known_kernel(entry, fix, message, rates, extra, mine, *again):
    modes = rates.shape[0]
    rate = rates[...]
    weight = extra[:modes] * jnp.sqrt(rate)
    lead = jnp.sum(weight * jnp.exp(rate), axis=0, keepdims=True)
    pieces = (
        entry[...],
        jnp.concatenate([fix[...], jnp.zeros_like(fix)], axis=0),
        message[modes : modes + SUBS],
        rate,
        weight * jnp.exp(-rate),
        jnp.concatenate([extra[modes : modes + 1], lead, jnp.zeros((SUBS - 2, rate.shape[1]), F32)], axis=0),
    )
    for target in (mine, *again[:1]):
        at = 0
        for piece in pieces:
            target[at : at + piece.shape[0]] = piece
            at += piece.shape[0]
    for target in again[1:]:
        target[...] = message[...]


def join(first, second, rates, rows):
    modes = rates.shape[0]
    start = second[modes : modes + SUBS]
    end = first[modes + SUBS :]
    added = start[0:2] * end[2:4] + end[0:2] * (start[2:4] + end[2:4])
    entering = first[:modes] + jnp.exp(rates) * added[0:1] + jnp.exp(2.0 * rates) * added[1:2]
    state = jnp.exp(-rates * float(rows)) * entering + second[:modes]
    both = jnp.concatenate([state, first[modes : modes + SUBS], second[modes + SUBS :]], axis=0)
    return both, entering, jnp.concatenate([added, end[4:6]], axis=0)


def scan_blocks(held, rates, rows, steps, level):
    block = lax.axis_index("seq")
    rounds = lax.axis_size("seq").bit_length() - 1
    message, entry, fix = held

    def place(level):
        upper = jnp.bitwise_and(jnp.right_shift(block, level), 1) == 1
        ahead = jnp.bitwise_and(block, (1 << level) - 1)
        return upper, ahead

    def ordered(upper, mine, other):
        return jnp.where(upper, other, mine), jnp.where(upper, mine, other)

    def enter(level, entry, fix, entering, added):
        upper, ahead = place(level)
        decay = jnp.exp(-rates * (ahead.astype(F32) * float(rows)))
        entry = jnp.where(upper, entry + decay * entering, entry)
        return entry, jnp.where(jnp.logical_and(upper, ahead == 0), added, fix)

    for masks in steps:
        if level >= rounds:
            break
        others = [seq_swap(message, mask) for mask in masks]
        upper, _ = place(level)
        message, entering, added = join(*ordered(upper, message, others[0]), rates, rows << level)
        entry, fix = enter(level, entry, fix, entering, added)
        if len(masks) == 3:
            pair, _, _ = join(*ordered(upper, others[1], others[2]), rates, rows << level)
            upper, _ = place(level + 1)
            message, entering, added = join(*ordered(upper, message, pair), rates, rows << (level + 1))
            entry, fix = enter(level + 1, entry, fix, entering, added)
        level += 1 if len(masks) == 1 else 2
    return message, entry, fix


def body(tokens, norm_gain, w_in, short_filter, rates, residues, skip_gain, w_out):
    rows, width = tokens.shape
    channels = w_in.shape[2]
    modes = rates.shape[0]
    far = ch_swap(tokens, 2)
    side = ch_swap(tokens, 1)
    mine = (jnp.transpose(w_in, (1, 0, 2)), short_filter, rates)
    staged = (tokens, norm_gain.reshape(-1, LANES))
    for array in mine:
        staged += (array, ch_swap(array, 1))
    kept = (0, 1, *range(2, len(staged), 2))
    staged = pl.pallas_call(
        stage_kernel,
        out_shape=tuple(jax.ShapeDtypeStruct(staged[i].shape, staged[i].dtype) for i in kept),
        in_specs=[pl.BlockSpec(memory_space=pl.ANY)] * len(staged),
        out_specs=tuple(vmem_specs(len(kept))),
        scratch_shapes=[pltpu.SemaphoreType.DMA((len(kept),))],
        compiler_params=pltpu.CompilerParams(vmem_limit_bytes=STAGE_VMEM),
        name="stage",
    )(*staged)
    far, staged = lax.optimization_barrier((far, staged))
    own_v, gain_v, w_in_v, taps_v, rates_v = staged
    side_far = ch_swap(far, 1)
    queries, gated, message = pl.pallas_call(
        front_kernel,
        out_shape=(
            jax.ShapeDtypeStruct((rows, channels), F32),
            jax.ShapeDtypeStruct((rows, channels), F32),
            jax.ShapeDtypeStruct((modes + 2 * SUBS, channels), F32),
        ),
        in_specs=vmem_specs(8),
        out_specs=tuple(vmem_specs(3)),
        scratch_shapes=[pltpu.VMEM((3 * channels // LANES, rows + HALO, LANES), F32)],
        compiler_params=pltpu.CompilerParams(vmem_limit_bytes=FRONT_VMEM),
        cost_estimate=pl.CostEstimate(flops=1_000_000, bytes_accessed=1_000, transcendentals=0),
        name="front",
    )(own_v, far, side, side_far, gain_v, w_in_v, taps_v, rates_v)
    skip = skip_gain.reshape(1, channels)
    pack, extra, w_out_v = pl.pallas_call(
        scan_kernel,
        out_shape=(
            jax.ShapeDtypeStruct((3, rows, channels), BF16),
            jax.ShapeDtypeStruct((modes + SUBS, channels), F32),
            jax.ShapeDtypeStruct(w_out.shape, BF16),
        ),
        in_specs=vmem_specs(9),
        out_specs=tuple(vmem_specs(3)),
        scratch_shapes=[pltpu.VMEM((rows, channels), F32)],
        compiler_params=pltpu.CompilerParams(vmem_limit_bytes=SCAN_VMEM),
        cost_estimate=pl.CostEstimate(flops=2_000_000_000, bytes_accessed=1_000_000, transcendentals=0),
        name="scan",
    )(queries, gated, rates_v, residues, ch_swap(residues, 1), skip, ch_swap(skip, 1), w_out, ch_swap(w_out, 1))
    held = (message, jnp.zeros_like(rates_v), jnp.zeros((4, channels), F32))
    held = scan_blocks(held, rates_v, rows, SCAN_FIRST[:1], 0)
    held, pack = lax.optimization_barrier((held, pack))
    pack_far = ch_swap(pack, 2)
    held = scan_blocks(held, rates_v, rows, SCAN_FIRST[1:], 1)
    row_shape = jax.ShapeDtypeStruct((3 * modes + 3 * SUBS, channels), F32)

    def known(*operands, copies=False):
        out_shape = (row_shape, row_shape, jax.ShapeDtypeStruct(message.shape, F32))[: 3 if copies else 1]
        return pl.pallas_call(
            known_kernel,
            out_shape=out_shape,
            in_specs=vmem_specs(5),
            out_specs=tuple(vmem_specs(len(out_shape))),
            compiler_params=pltpu.CompilerParams(vmem_limit_bytes=STAGE_VMEM),
            name="known",
        )(*operands, rates_v, extra)

    def later(_, now):
        message, _, mine, _ = now
        held = (message, mine[:modes], mine[modes : modes + 4])
        message, entry, fix = scan_blocks(held, rates_v, rows, SCAN_LATER, len(SCAN_FIRST))
        (mine,) = known(entry, fix, message)
        other = seq_swap(message, SCAN_LAST)
        other_far = seq_swap(message, SCAN_LAST, 1)
        return other, other_far, mine, ch_swap(mine, 2)

    once = jnp.minimum(lax.axis_index("seq") + 1, 1)
    message, entry, fix = held
    mine, mine_again, message_again = known(entry, fix, message, copies=True)
    now = lax.fori_loop(0, once, later, (message, message_again, mine, mine_again))
    (other, other_far, mine, mine_far), pack_far = lax.optimization_barrier((now, pack_far))
    scratch = [pltpu.VMEM((modes + SUBS, channels), F32), pltpu.VMEM((channels // LANES, rows, LANES), F32)]
    share = pl.pallas_call(
        near_kernel,
        out_shape=jax.ShapeDtypeStruct((2, rows, width), F32),
        in_specs=vmem_specs(4),
        out_specs=vmem_specs(1)[0],
        scratch_shapes=scratch,
        compiler_params=pltpu.CompilerParams(vmem_limit_bytes=BACK_VMEM),
        cost_estimate=pl.CostEstimate(flops=900_000_000, bytes_accessed=4_000_000, transcendentals=0),
        name="near",
    )(pack, mine, other, w_out_v)
    kept, sent = pl.pallas_call(
        far_kernel,
        out_shape=(
            jax.ShapeDtypeStruct((rows, width), F32),
            jax.ShapeDtypeStruct((rows, width), BF16),
        ),
        in_specs=vmem_specs(4),
        out_specs=tuple(vmem_specs(2)),
        scratch_shapes=scratch,
        compiler_params=pltpu.CompilerParams(vmem_limit_bytes=BACK_VMEM),
        cost_estimate=pl.CostEstimate(flops=900_000_000, bytes_accessed=4_000_000, transcendentals=0),
        name="far",
    )(pack_far, mine_far, other_far, share)
    return (kept + ch_swap(sent, 1).astype(F32)).astype(BF16)


def solution(mesh):
    return jax.shard_map(
        body,
        mesh=mesh,
        in_specs=(
            P("seq", "ch"),
            P(),
            P(None, None, "ch"),
            P(None, None, "ch"),
            P(None, "ch"),
            P(None, "ch"),
            P("ch"),
            P("ch", None),
        ),
        out_specs=P("seq", "ch"),
        check_vma=False,
    )
```

```python
import jax
import jax.numpy as jnp
from jax import lax
from jax.experimental import pallas as pl
from jax.experimental.pallas import tpu as pltpu
from jax.sharding import PartitionSpec as P

EPSILON = 1e-06
F32 = jnp.float32
BF16 = jnp.bfloat16
LANES = 128
SUBS = 8
HALO = 16
STAGE_VMEM = 1024 * 1024
FRONT_VMEM = 8 * 1024 * 1024
SCAN_VMEM = 2 * 1024 * 1024
BACK_VMEM = 4 * 1024 * 1024

SCAN_FIRST = ((1,), (3,))
SCAN_LATER = ((4, 8, 12), (24,))
SCAN_LAST = 32

CROSSED = 0b101101


def ch_swap(array, mask):
    return lax.ppermute(array, "ch", [(i, i ^ mask) for i in range(lax.axis_size("ch"))])


def crosses(mask):
    return bin(mask & CROSSED).count("1") % 2


def crossed(block):
    bits = [jnp.right_shift(block, bit) for bit in range(CROSSED.bit_length()) if CROSSED >> bit & 1]
    total = bits[0]
    for bit in bits[1:]:
        total = jnp.bitwise_xor(total, bit)
    return jnp.bitwise_and(total, 1) == 1


def seq_swap(array, mask, chip=0):
    blocks, chs = lax.axis_size("seq"), lax.axis_size("ch")
    turn = 2 * chip ^ crosses(mask)
    pairs = [(chs * b + c, chs * (b ^ mask) + (c ^ turn)) for b in range(blocks) for c in range(chs)]
    return lax.ppermute(array, ("seq", "ch"), pairs)


def vmem_specs(count):
    return [pl.BlockSpec(memory_space=pltpu.VMEM)] * count


def row(ref, index, lanes):
    return jnp.broadcast_to(ref[pl.ds(index, 1), lanes], (SUBS, LANES))


def tree_sum(terms):
    while len(terms) > 1:
        terms = [sum(terms[i : i + 2][1:], terms[i]) for i in range(0, len(terms), 2)]
    return terms[0]


def stage_kernel(*refs):
    (own, gain), pairs, targets, sems = refs[:2], refs[2:8], refs[8:13], refs[13]
    swapped = crossed(lax.axis_index("seq"))

    def copy_all(sources):
        copies = [pltpu.make_async_copy(src, dst, sems.at[i]) for i, (src, dst) in enumerate(zip(sources, targets))]
        for copy in copies:
            copy.start()
        for copy in copies:
            copy.wait()

    @pl.when(swapped)
    def _():
        copy_all((own, gain, *pairs[1::2]))

    @pl.when(jnp.logical_not(swapped))
    def _():
        copy_all((own, gain, *pairs[::2]))


def front_kernel(
    own, far, side, side_far, gain, w_in, taps, rates,
    queries, gated, message, projected,
):
    me = lax.axis_index("ch")
    rows, width = own.shape
    span = rows // SUBS
    modes = rates.shape[0]
    tiles = width // LANES
    square = jnp.zeros((rows, LANES), F32)
    blocks = (own, side, far, side_far)
    for block in blocks:
        for lane in range(0, width, LANES):
            piece = block[:, lane : lane + LANES].astype(F32)
            square = square + piece * piece
    scale = lax.rsqrt(jnp.sum(square, axis=1, keepdims=True) * (1.0 / (4 * width)) + EPSILON)
    normed = []
    for order, block in enumerate(blocks):
        part = jnp.bitwise_xor(me, order)
        pieces = [
            block[:, tile * LANES : (tile + 1) * LANES].astype(F32) * scale * gain[pl.ds(part * tiles + tile, 1), :]
            for tile in range(tiles)
        ]
        normed.append(jnp.concatenate(pieces, axis=1).astype(BF16))
    for group in range(3):
        total = jnp.zeros((rows, width), F32)
        for order in range(4):
            start = pl.multiple_of(jnp.bitwise_xor(me, order) * width, width)
            total = total + jnp.dot(
                normed[order], w_in[group, pl.ds(start, width), :], preferred_element_type=F32
            )
        total = total.astype(BF16).astype(F32)
        for tile in range(tiles):
            projected[group * tiles + tile, :HALO] = jnp.zeros((HALO, LANES), F32)
            projected[group * tiles + tile, HALO:] = total[:, tile * LANES : (tile + 1) * LANES]

    sub = lax.broadcasted_iota(jnp.int32, (SUBS, LANES), 0)
    message[...] = jnp.zeros_like(message)
    for tile in range(tiles):
        lanes = pl.ds(tile * LANES, LANES)
        rate = [row(rates, m, lanes) for m in range(modes)]
        decay = [jnp.exp(-r) for r in rate]
        tap = [[jnp.broadcast_to(taps[s, pl.ds(g, 1), lanes], (SUBS, LANES)) for s in range(3)] for g in range(3)]

        def read(start, group):
            return projected[group * tiles + tile, pl.ds(start, SUBS, stride=span), :]

        def step(index, held):
            before, state = held
            now = [read(HALO + index, g) for g in range(3)]
            filtered = [
                tap[g][0] * now[g] + tap[g][1] * before[0][g] + tap[g][2] * before[1][g] for g in range(3)
            ]
            product = filtered[1] * filtered[2]
            at = pl.ds(pl.multiple_of(index * SUBS, SUBS), SUBS)
            queries[at, lanes] = filtered[0]
            gated[at, lanes] = product
            return ((now, before[0]), [decay[m] * state[m] + product for m in range(modes)])

        first = ([read(HALO - 1, g) for g in range(3)], [read(HALO - 2, g) for g in range(3)])
        zeros = [jnp.zeros((SUBS, LANES), F32)] * modes
        _, state = lax.fori_loop(0, span, step, (first, zeros), unroll=8)
        for m in range(modes):
            upto = state[m] * jnp.exp(rate[m] * (float(span) * (sub - (SUBS - 1)).astype(F32)))
            message[pl.ds(m, 1), lanes] = jnp.sum(upto, axis=0, keepdims=True)
        for group in range(3):
            t = [taps[s, pl.ds(group, 1), lanes] for s in range(3)]
            p = [projected[group * tiles + tile, pl.ds(HALO + i, 1), :] for i in (0, 1, rows - 2, rows - 1)]
            if group > 0:
                message[pl.ds(modes + 2 * group - 2, 1), lanes] = t[0] * p[0]
                message[pl.ds(modes + 2 * group - 1, 1), lanes] = t[0] * p[1] + t[1] * p[0]
            to = modes + SUBS + 2 * ((group - 1) % 3)
            message[pl.ds(to, 1), lanes] = t[1] * p[3] + t[2] * p[2]
            message[pl.ds(to + 1, 1), lanes] = t[2] * p[3]


def scan_kernel(
    queries, gated, rates, residues, residues_side, skip, skip_side, w_out, w_out_side, pack, extra, w_out_v, local, sems
):
    rows, width = gated.shape
    modes = rates.shape[0]
    swapped = crossed(lax.axis_index("seq"))

    other = 1 - jnp.right_shift(lax.axis_index("ch"), 1)

    def projection_copies(projection):
        pairs = [(projection, w_out_v)]
        for column in range(2):
            start = pl.multiple_of((2 * other + column) * width, width)
            pairs.append((projection.at[:, pl.ds(start, width)], pack.at[2, pl.ds(column * width, width), :]))
        return [pltpu.make_async_copy(src, dst, sems.at[i]) for i, (src, dst) in enumerate(pairs)]

    def keep(weights, direct, projection):
        for copy in projection_copies(projection):
            copy.start()
        extra[:modes] = weights[...]
        extra[modes:] = jnp.concatenate([direct[...], jnp.zeros((SUBS - 1, width), F32)], axis=0)

    @pl.when(swapped)
    def _():
        keep(residues_side, skip_side, w_out_side)

    @pl.when(jnp.logical_not(swapped))
    def _():
        keep(residues, skip, w_out)

    span = rows // SUBS
    sub = lax.broadcasted_iota(jnp.int32, (SUBS, LANES), 0)
    for lane in range(0, width, LANES):
        lanes = pl.ds(lane, LANES)
        rate = [row(rates, m, lanes) for m in range(modes)]
        decay = [jnp.exp(-r) for r in rate]
        weight = [row(extra, m, lanes) * jnp.sqrt(rate[m]) for m in range(modes)]
        skip_row = row(extra, modes, lanes)

        def step(index, state):
            at = pl.ds(pl.multiple_of(index * SUBS, SUBS), SUBS)
            product = gated[at, lanes]
            state = [decay[m] * state[m] + product for m in range(modes)]
            local[at, lanes] = tree_sum([weight[m] * state[m] for m in range(modes)] + [skip_row * product])
            return state

        state = lax.fori_loop(0, span, step, [jnp.zeros((SUBS, LANES), F32)] * modes, unroll=8)
        brought = []
        for m in range(modes):
            upto = state[m]
            for reach in (1, 2, 4):
                moved = pltpu.roll(upto, reach, 0) * jnp.exp(rate[m] * (-float(span * reach)))
                upto = upto + jnp.where(sub >= reach, moved, 0.0)
            brought.append(weight[m] * decay[m] * jnp.where(sub >= 1, pltpu.roll(upto, 1, 0), 0.0))

        def add(index, held):
            both = []
            for half in range(2):
                at = pl.ds(pl.multiple_of((2 * index + half) * SUBS, SUBS), SUBS)
                both.append(tree_sum(list(held) + [local[at, lanes]]))
                held = [decay[m] * held[m] for m in range(modes)]
            at = pl.ds(pl.multiple_of(index * 2 * SUBS, 2 * SUBS), 2 * SUBS)
            pack[0, at, lanes] = queries[at, lanes].astype(BF16)
            pack[1, at, lanes] = jnp.concatenate(both, axis=0).astype(BF16)
            return held

        lax.fori_loop(0, span // 2, add, brought, unroll=2)

    @pl.when(swapped)
    def _():
        for copy in projection_copies(w_out_side):
            copy.wait()

    @pl.when(jnp.logical_not(swapped))
    def _():
        for copy in projection_copies(w_out):
            copy.wait()


def mix(read, mine, other, entry, mixed):
    tiles, rows = mixed.shape[:2]
    span = rows // SUBS
    modes = (mine.shape[0] - 3 * SUBS) // 3
    block, half = lax.axis_index("seq"), lax.axis_size("seq") // 2
    upper = (block >= half).astype(F32)
    first = (block == half).astype(F32)
    passed = (jnp.maximum(block - half, 0) * rows).astype(F32)
    fix, start, end = mine[modes : modes + 4], mine[modes + SUBS : modes + 2 * SUBS], other[modes + SUBS :]
    rates = mine[modes + 2 * SUBS : 2 * modes + 2 * SUBS]
    weights = mine[2 * modes + 2 * SUBS : 3 * modes + 2 * SUBS]
    skip, lead = mine[3 * modes + 2 * SUBS : 3 * modes + 2 * SUBS + 1], mine[3 * modes + 2 * SUBS + 1 : 3 * modes + 2 * SUBS + 2]
    added = start[0:2] * end[2:4] + end[0:2] * (start[2:4] + end[2:4])
    joined = other[:modes] + jnp.exp(rates) * added[0:1] + jnp.exp(2.0 * rates) * added[1:2]
    entry[:modes] = weights * (mine[:modes] + upper * jnp.exp(-rates * passed) * joined)
    added = fix[0:2] + first * added
    entry[modes : modes + 1] = skip * added[0:1] - lead * added[1:2]
    entry[modes + 1 : modes + 2] = skip * added[1:2]
    entry[modes + 2 : modes + 4] = fix[2:4] + first * end[4:6]
    sub = lax.broadcasted_iota(jnp.int32, (SUBS, LANES), 0)
    for tile in range(tiles):
        lanes = pl.ds(tile * LANES, LANES)
        rate = [row(mine, modes + 2 * SUBS + m, lanes) for m in range(modes)]
        decay = [jnp.exp(-r) for r in rate]
        state = [jnp.exp(rate[m] * sub.astype(F32) * (-float(span))) * row(entry, m, lanes) for m in range(modes)]
        more = [row(entry, modes + i, lanes) for i in range(4)]

        def pair(index, held, more=None):
            at = pl.ds(pl.multiple_of(index * 2 * SUBS, 2 * SUBS), 2 * SUBS)
            query, value = (part.astype(F32) for part in read(at, lanes))
            for half in range(2):
                v, q = value[half * SUBS : (half + 1) * SUBS], query[half * SUBS : (half + 1) * SUBS]
                if more is not None:
                    v = v + jnp.where(sub == 0, more[half], 0.0)
                    q = q + jnp.where(sub == 0, more[2 + half], 0.0)
                token = 2 * index + half
                mixed[tile, pl.ds(token, SUBS, stride=span), :] = q * tree_sum(list(held) + [v])
                held = [decay[m] * held[m] for m in range(modes)]
            return held

        state = pair(0, state, more)
        lax.fori_loop(1, span // 2, pair, state, unroll=2)
    return jnp.concatenate([mixed[tile] for tile in range(tiles)], axis=1).astype(BF16)


def near_kernel(pack, mine, other, w_out, share, entry, mixed):
    me = lax.axis_index("ch")
    chip, core = jnp.right_shift(me, 1), jnp.bitwise_and(me, 1)
    width = pack.shape[2]
    part = mix(lambda at, lanes: (pack[0, at, lanes], pack[1, at, lanes]), mine, other, entry, mixed)
    for slot, column in enumerate((1 - core, core)):
        start = pl.multiple_of((2 * chip + column) * width, width)
        share[slot] = jnp.dot(part, w_out[:, pl.ds(start, width)], preferred_element_type=F32)


def far_kernel(pack, mine, other, share, kept, sent, entry, mixed):
    core = jnp.bitwise_and(lax.axis_index("ch"), 1)
    width = pack.shape[2]
    part = mix(lambda at, lanes: (pack[0, at, lanes], pack[1, at, lanes]), mine, other, entry, mixed)
    for slot, (target, column) in enumerate(((sent, 1 - core), (kept, core))):
        start = pl.multiple_of(column * width, width)
        total = share[slot] + jnp.dot(part, pack[2, pl.ds(start, width), :], preferred_element_type=F32)
        target[...] = total.astype(target.dtype)


def known_kernel(entry, fix, message, rates, extra, mine, *again):
    modes = rates.shape[0]
    rate = rates[...]
    weight = extra[:modes] * jnp.sqrt(rate)
    lead = jnp.sum(weight * jnp.exp(rate), axis=0, keepdims=True)
    pieces = (
        entry[...],
        jnp.concatenate([fix[...], jnp.zeros_like(fix)], axis=0),
        message[modes : modes + SUBS],
        rate,
        weight * jnp.exp(-rate),
        jnp.concatenate([extra[modes : modes + 1], lead, jnp.zeros((SUBS - 2, rate.shape[1]), F32)], axis=0),
    )
    for target in (mine, *again[:1]):
        at = 0
        for piece in pieces:
            target[at : at + piece.shape[0]] = piece
            at += piece.shape[0]
    for target in again[1:]:
        target[...] = message[...]


def join(first, second, rates, rows):
    modes = rates.shape[0]
    start = second[modes : modes + SUBS]
    end = first[modes + SUBS :]
    added = start[0:2] * end[2:4] + end[0:2] * (start[2:4] + end[2:4])
    entering = first[:modes] + jnp.exp(rates) * added[0:1] + jnp.exp(2.0 * rates) * added[1:2]
    state = jnp.exp(-rates * float(rows)) * entering + second[:modes]
    both = jnp.concatenate([state, first[modes : modes + SUBS], second[modes + SUBS :]], axis=0)
    return both, entering, jnp.concatenate([added, end[4:6]], axis=0)


def scan_blocks(held, rates, rows, steps, level):
    block = lax.axis_index("seq")
    rounds = lax.axis_size("seq").bit_length() - 1
    message, entry, fix = held

    def place(level):
        upper = jnp.bitwise_and(jnp.right_shift(block, level), 1) == 1
        ahead = jnp.bitwise_and(block, (1 << level) - 1)
        return upper, ahead

    def ordered(upper, mine, other):
        return jnp.where(upper, other, mine), jnp.where(upper, mine, other)

    def enter(level, entry, fix, entering, added):
        upper, ahead = place(level)
        decay = jnp.exp(-rates * (ahead.astype(F32) * float(rows)))
        entry = jnp.where(upper, entry + decay * entering, entry)
        return entry, jnp.where(jnp.logical_and(upper, ahead == 0), added, fix)

    for masks in steps:
        if level >= rounds:
            break
        others = [seq_swap(message, mask) for mask in masks]
        upper, _ = place(level)
        message, entering, added = join(*ordered(upper, message, others[0]), rates, rows << level)
        entry, fix = enter(level, entry, fix, entering, added)
        if len(masks) == 3:
            pair, _, _ = join(*ordered(upper, others[1], others[2]), rates, rows << level)
            upper, _ = place(level + 1)
            message, entering, added = join(*ordered(upper, message, pair), rates, rows << (level + 1))
            entry, fix = enter(level + 1, entry, fix, entering, added)
        level += 1 if len(masks) == 1 else 2
    return message, entry, fix


def body(tokens, norm_gain, w_in, short_filter, rates, residues, skip_gain, w_out):
    rows, width = tokens.shape
    channels = w_in.shape[2]
    modes = rates.shape[0]
    far = ch_swap(tokens, 2)
    side = ch_swap(tokens, 1)
    mine = (jnp.transpose(w_in, (1, 0, 2)), short_filter, rates)
    staged = (tokens, norm_gain.reshape(-1, LANES))
    for array in mine:
        staged += (array, ch_swap(array, 1))
    kept = (0, 1, *range(2, len(staged), 2))
    staged = pl.pallas_call(
        stage_kernel,
        out_shape=tuple(jax.ShapeDtypeStruct(staged[i].shape, staged[i].dtype) for i in kept),
        in_specs=[pl.BlockSpec(memory_space=pl.ANY)] * len(staged),
        out_specs=tuple(vmem_specs(len(kept))),
        scratch_shapes=[pltpu.SemaphoreType.DMA((len(kept),))],
        compiler_params=pltpu.CompilerParams(vmem_limit_bytes=STAGE_VMEM),
        name="stage",
    )(*staged)
    far, staged = lax.optimization_barrier((far, staged))
    own_v, gain_v, w_in_v, taps_v, rates_v = staged
    side_far = ch_swap(far, 1)
    queries, gated, message = pl.pallas_call(
        front_kernel,
        out_shape=(
            jax.ShapeDtypeStruct((rows, channels), F32),
            jax.ShapeDtypeStruct((rows, channels), F32),
            jax.ShapeDtypeStruct((modes + 2 * SUBS, channels), F32),
        ),
        in_specs=vmem_specs(8),
        out_specs=tuple(vmem_specs(3)),
        scratch_shapes=[pltpu.VMEM((3 * channels // LANES, rows + HALO, LANES), F32)],
        compiler_params=pltpu.CompilerParams(vmem_limit_bytes=FRONT_VMEM),
        cost_estimate=pl.CostEstimate(flops=1_000_000, bytes_accessed=1_000, transcendentals=0),
        name="front",
    )(own_v, far, side, side_far, gain_v, w_in_v, taps_v, rates_v)
    skip = skip_gain.reshape(1, channels)
    pack, extra, w_out_v = pl.pallas_call(
        scan_kernel,
        out_shape=(
            jax.ShapeDtypeStruct((3, rows, channels), BF16),
            jax.ShapeDtypeStruct((modes + SUBS, channels), F32),
            jax.ShapeDtypeStruct(w_out.shape, BF16),
        ),
        in_specs=vmem_specs(7) + [pl.BlockSpec(memory_space=pl.ANY)] * 2,
        out_specs=tuple(vmem_specs(3)),
        scratch_shapes=[pltpu.VMEM((rows, channels), F32), pltpu.SemaphoreType.DMA((3,))],
        compiler_params=pltpu.CompilerParams(vmem_limit_bytes=SCAN_VMEM),
        cost_estimate=pl.CostEstimate(flops=2_000_000_000, bytes_accessed=1_000_000, transcendentals=0),
        name="scan",
    )(queries, gated, rates_v, residues, ch_swap(residues, 1), skip, ch_swap(skip, 1), w_out, ch_swap(w_out, 1))
    held = (message, jnp.zeros_like(rates_v), jnp.zeros((4, channels), F32))
    held = scan_blocks(held, rates_v, rows, SCAN_FIRST[:1], 0)
    held, pack = lax.optimization_barrier((held, pack))
    pack_far = ch_swap(pack, 2)
    held = scan_blocks(held, rates_v, rows, SCAN_FIRST[1:], 1)
    row_shape = jax.ShapeDtypeStruct((3 * modes + 3 * SUBS, channels), F32)

    def known(*operands, copies=False):
        out_shape = (row_shape, row_shape, jax.ShapeDtypeStruct(message.shape, F32))[: 3 if copies else 1]
        return pl.pallas_call(
            known_kernel,
            out_shape=out_shape,
            in_specs=vmem_specs(5),
            out_specs=tuple(vmem_specs(len(out_shape))),
            compiler_params=pltpu.CompilerParams(vmem_limit_bytes=STAGE_VMEM),
            name="known",
        )(*operands, rates_v, extra)

    def later(_, now):
        message, _, mine, _ = now
        held = (message, mine[:modes], mine[modes : modes + 4])
        message, entry, fix = scan_blocks(held, rates_v, rows, SCAN_LATER, len(SCAN_FIRST))
        (mine,) = known(entry, fix, message)
        other = seq_swap(message, SCAN_LAST)
        other_far = seq_swap(message, SCAN_LAST, 1)
        return other, other_far, mine, ch_swap(mine, 2)

    once = jnp.minimum(lax.axis_index("seq") + 1, 1)
    message, entry, fix = held
    mine, mine_again, message_again = known(entry, fix, message, copies=True)
    now = lax.fori_loop(0, once, later, (message, message_again, mine, mine_again))
    (other, other_far, mine, mine_far), pack_far = lax.optimization_barrier((now, pack_far))
    scratch = [pltpu.VMEM((modes + SUBS, channels), F32), pltpu.VMEM((channels // LANES, rows, LANES), F32)]
    share = pl.pallas_call(
        near_kernel,
        out_shape=jax.ShapeDtypeStruct((2, rows, width), F32),
        in_specs=vmem_specs(4),
        out_specs=vmem_specs(1)[0],
        scratch_shapes=scratch,
        compiler_params=pltpu.CompilerParams(vmem_limit_bytes=BACK_VMEM),
        cost_estimate=pl.CostEstimate(flops=900_000_000, bytes_accessed=4_000_000, transcendentals=0),
        name="near",
    )(pack, mine, other, w_out_v)
    kept, sent = pl.pallas_call(
        far_kernel,
        out_shape=(
            jax.ShapeDtypeStruct((rows, width), F32),
            jax.ShapeDtypeStruct((rows, width), BF16),
        ),
        in_specs=vmem_specs(4),
        out_specs=tuple(vmem_specs(2)),
        scratch_shapes=scratch,
        compiler_params=pltpu.CompilerParams(vmem_limit_bytes=BACK_VMEM),
        cost_estimate=pl.CostEstimate(flops=900_000_000, bytes_accessed=4_000_000, transcendentals=0),
        name="far",
    )(pack_far, mine_far, other_far, share)
    return (kept + ch_swap(sent, 1).astype(F32)).astype(BF16)


def solution(mesh):
    return jax.shard_map(
        body,
        mesh=mesh,
        in_specs=(
            P("seq", "ch"),
            P(),
            P(None, None, "ch"),
            P(None, None, "ch"),
            P(None, "ch"),
            P(None, "ch"),
            P("ch"),
            P("ch", None),
        ),
        out_specs=P("seq", "ch"),
        check_vma=False,
    )
```

```python
import jax
import jax.numpy as jnp
from jax import lax
from jax.experimental import pallas as pl
from jax.experimental.pallas import tpu as pltpu
from jax.sharding import PartitionSpec as P

EPSILON = 1e-06
F32 = jnp.float32
BF16 = jnp.bfloat16
LANES = 128
SUBS = 8
HALO = 16
STAGE_VMEM = 1024 * 1024
FRONT_VMEM = 8 * 1024 * 1024
SCAN_VMEM = 2 * 1024 * 1024
BACK_VMEM = 4 * 1024 * 1024

SCAN_FIRST = ((1,), (3,))
SCAN_LATER = ((4, 8, 12), (24,))
SCAN_LAST = 32

CROSSED = 0b101101


def ch_swap(array, mask):
    return lax.ppermute(array, "ch", [(i, i ^ mask) for i in range(lax.axis_size("ch"))])


def crosses(mask):
    return bin(mask & CROSSED).count("1") % 2


def crossed(block):
    bits = [jnp.right_shift(block, bit) for bit in range(CROSSED.bit_length()) if CROSSED >> bit & 1]
    total = bits[0]
    for bit in bits[1:]:
        total = jnp.bitwise_xor(total, bit)
    return jnp.bitwise_and(total, 1) == 1


def seq_swap(array, mask, chip=0):
    blocks, chs = lax.axis_size("seq"), lax.axis_size("ch")
    turn = 2 * chip ^ crosses(mask)
    pairs = [(chs * b + c, chs * (b ^ mask) + (c ^ turn)) for b in range(blocks) for c in range(chs)]
    return lax.ppermute(array, ("seq", "ch"), pairs)


def vmem_specs(count):
    return [pl.BlockSpec(memory_space=pltpu.VMEM)] * count


def row(ref, index, lanes):
    return jnp.broadcast_to(ref[pl.ds(index, 1), lanes], (SUBS, LANES))


def tree_sum(terms):
    while len(terms) > 1:
        terms = [sum(terms[i : i + 2][1:], terms[i]) for i in range(0, len(terms), 2)]
    return terms[0]


def stage_kernel(*refs):
    (own, gain), pairs, targets, sems = refs[:2], refs[2:8], refs[8:13], refs[13]
    swapped = crossed(lax.axis_index("seq"))

    def copy_all(sources):
        copies = [pltpu.make_async_copy(src, dst, sems.at[i]) for i, (src, dst) in enumerate(zip(sources, targets))]
        for copy in copies:
            copy.start()
        for copy in copies:
            copy.wait()

    @pl.when(swapped)
    def _():
        copy_all((own, gain, *pairs[1::2]))

    @pl.when(jnp.logical_not(swapped))
    def _():
        copy_all((own, gain, *pairs[::2]))


def front_kernel(
    own, far, side, side_far, gain, w_in, taps, rates,
    queries, gated, message, projected,
):
    me = lax.axis_index("ch")
    rows, width = own.shape
    span = rows // SUBS
    modes = rates.shape[0]
    tiles = width // LANES
    square = jnp.zeros((rows, LANES), F32)
    blocks = (own, side, far, side_far)
    for block in blocks:
        for lane in range(0, width, LANES):
            piece = block[:, lane : lane + LANES].astype(F32)
            square = square + piece * piece
    scale = lax.rsqrt(jnp.sum(square, axis=1, keepdims=True) * (1.0 / (4 * width)) + EPSILON)
    normed = []
    for order, block in enumerate(blocks):
        part = jnp.bitwise_xor(me, order)
        pieces = [
            block[:, tile * LANES : (tile + 1) * LANES].astype(F32) * scale * gain[pl.ds(part * tiles + tile, 1), :]
            for tile in range(tiles)
        ]
        normed.append(jnp.concatenate(pieces, axis=1).astype(BF16))
    for group in range(3):
        total = jnp.zeros((rows, width), F32)
        for order in range(4):
            start = pl.multiple_of(jnp.bitwise_xor(me, order) * width, width)
            total = total + jnp.dot(
                normed[order], w_in[group, pl.ds(start, width), :], preferred_element_type=F32
            )
        total = total.astype(BF16).astype(F32)
        for tile in range(tiles):
            projected[group * tiles + tile, :HALO] = jnp.zeros((HALO, LANES), F32)
            projected[group * tiles + tile, HALO : HALO + rows] = total[:, tile * LANES : (tile + 1) * LANES]

    sub = lax.broadcasted_iota(jnp.int32, (SUBS, LANES), 0)
    message[...] = jnp.zeros_like(message)
    for tile in range(tiles):
        lanes = pl.ds(tile * LANES, LANES)
        rate = [row(rates, m, lanes) for m in range(modes)]
        decay = [jnp.exp(-r) for r in rate]
        tap = [[jnp.broadcast_to(taps[s, pl.ds(g, 1), lanes], (SUBS, LANES)) for s in range(3)] for g in range(3)]

        def read(start, group):
            return projected[group * tiles + tile, pl.ds(start, SUBS, stride=span), :]

        def step(index, held):
            before, state = held
            now = [read(HALO + index, g) for g in range(3)]
            filtered = [
                tap[g][0] * now[g] + tap[g][1] * before[0][g] + tap[g][2] * before[1][g] for g in range(3)
            ]
            product = filtered[1] * filtered[2]
            at = pl.ds(pl.multiple_of(index * SUBS, SUBS), SUBS)
            queries[at, lanes] = filtered[0]
            gated[at, lanes] = product
            return ((now, before[0]), [decay[m] * state[m] + product for m in range(modes)])

        first = ([read(HALO - 1, g) for g in range(3)], [read(HALO - 2, g) for g in range(3)])
        zeros = [jnp.zeros((SUBS, LANES), F32)] * modes
        _, state = lax.fori_loop(0, span, step, (first, zeros), unroll=8)
        for m in range(modes):
            upto = state[m] * jnp.exp(rate[m] * (float(span) * (sub - (SUBS - 1)).astype(F32)))
            message[pl.ds(m, 1), lanes] = jnp.sum(upto, axis=0, keepdims=True)
        for group in range(3):
            t = [taps[s, pl.ds(group, 1), lanes] for s in range(3)]
            p = [projected[group * tiles + tile, pl.ds(HALO + i, 1), :] for i in (0, 1, rows - 2, rows - 1)]
            if group > 0:
                message[pl.ds(modes + 2 * group - 2, 1), lanes] = t[0] * p[0]
                message[pl.ds(modes + 2 * group - 1, 1), lanes] = t[0] * p[1] + t[1] * p[0]
            to = modes + SUBS + 2 * ((group - 1) % 3)
            message[pl.ds(to, 1), lanes] = t[1] * p[3] + t[2] * p[2]
            message[pl.ds(to + 1, 1), lanes] = t[2] * p[3]


def scan_kernel(
    queries, gated, rates, residues, residues_side, skip, skip_side, w_out, w_out_side, pack, extra, w_out_v, local, sems
):
    rows, width = gated.shape
    modes = rates.shape[0]
    swapped = crossed(lax.axis_index("seq"))

    other = 1 - jnp.right_shift(lax.axis_index("ch"), 1)

    def projection_copies(projection):
        pairs = [(projection, w_out_v)]
        for column in range(2):
            start = pl.multiple_of((2 * other + column) * width, width)
            pairs.append((projection.at[:, pl.ds(start, width)], pack.at[2, pl.ds(column * width, width), :]))
        return [pltpu.make_async_copy(src, dst, sems.at[i]) for i, (src, dst) in enumerate(pairs)]

    def keep(weights, direct, projection):
        for copy in projection_copies(projection):
            copy.start()
        extra[:modes] = weights[...]
        extra[modes:] = jnp.concatenate([direct[...], jnp.zeros((SUBS - 1, width), F32)], axis=0)

    @pl.when(swapped)
    def _():
        keep(residues_side, skip_side, w_out_side)

    @pl.when(jnp.logical_not(swapped))
    def _():
        keep(residues, skip, w_out)

    span = rows // SUBS
    sub = lax.broadcasted_iota(jnp.int32, (SUBS, LANES), 0)
    for lane in range(0, width, LANES):
        lanes = pl.ds(lane, LANES)
        rate = [row(rates, m, lanes) for m in range(modes)]
        decay = [jnp.exp(-r) for r in rate]
        weight = [row(extra, m, lanes) * jnp.sqrt(rate[m]) for m in range(modes)]
        skip_row = row(extra, modes, lanes)

        def step(index, state):
            at = pl.ds(pl.multiple_of(index * SUBS, SUBS), SUBS)
            product = gated[at, lanes]
            state = [decay[m] * state[m] + product for m in range(modes)]
            local[at, lanes] = tree_sum([weight[m] * state[m] for m in range(modes)] + [skip_row * product])
            return state

        state = lax.fori_loop(0, span, step, [jnp.zeros((SUBS, LANES), F32)] * modes, unroll=8)
        brought = []
        for m in range(modes):
            upto = state[m]
            for reach in (1, 2, 4):
                moved = pltpu.roll(upto, reach, 0) * jnp.exp(rate[m] * (-float(span * reach)))
                upto = upto + jnp.where(sub >= reach, moved, 0.0)
            brought.append(weight[m] * decay[m] * jnp.where(sub >= 1, pltpu.roll(upto, 1, 0), 0.0))

        def add(index, held):
            both = []
            for half in range(2):
                at = pl.ds(pl.multiple_of((2 * index + half) * SUBS, SUBS), SUBS)
                both.append(tree_sum(list(held) + [local[at, lanes]]))
                held = [decay[m] * held[m] for m in range(modes)]
            at = pl.ds(pl.multiple_of(index * 2 * SUBS, 2 * SUBS), 2 * SUBS)
            pack[0, at, lanes] = queries[at, lanes].astype(BF16)
            pack[1, at, lanes] = jnp.concatenate(both, axis=0).astype(BF16)
            return held

        lax.fori_loop(0, span // 2, add, brought, unroll=2)

    @pl.when(swapped)
    def _():
        for copy in projection_copies(w_out_side):
            copy.wait()

    @pl.when(jnp.logical_not(swapped))
    def _():
        for copy in projection_copies(w_out):
            copy.wait()


def mix(read, mine, other, entry, mixed):
    tiles, rows = mixed.shape[0], mixed.shape[1] * SUBS // (SUBS + 1)
    span = rows // SUBS
    modes = (mine.shape[0] - 3 * SUBS) // 3
    block, half = lax.axis_index("seq"), lax.axis_size("seq") // 2
    upper = (block >= half).astype(F32)
    first = (block == half).astype(F32)
    passed = (jnp.maximum(block - half, 0) * rows).astype(F32)
    fix, start, end = mine[modes : modes + 4], mine[modes + SUBS : modes + 2 * SUBS], other[modes + SUBS :]
    rates = mine[modes + 2 * SUBS : 2 * modes + 2 * SUBS]
    weights = mine[2 * modes + 2 * SUBS : 3 * modes + 2 * SUBS]
    skip, lead = mine[3 * modes + 2 * SUBS : 3 * modes + 2 * SUBS + 1], mine[3 * modes + 2 * SUBS + 1 : 3 * modes + 2 * SUBS + 2]
    added = start[0:2] * end[2:4] + end[0:2] * (start[2:4] + end[2:4])
    joined = other[:modes] + jnp.exp(rates) * added[0:1] + jnp.exp(2.0 * rates) * added[1:2]
    entry[:modes] = weights * (mine[:modes] + upper * jnp.exp(-rates * passed) * joined)
    added = fix[0:2] + first * added
    entry[modes : modes + 1] = skip * added[0:1] - lead * added[1:2]
    entry[modes + 1 : modes + 2] = skip * added[1:2]
    entry[modes + 2 : modes + 4] = fix[2:4] + first * end[4:6]
    sub = lax.broadcasted_iota(jnp.int32, (SUBS, LANES), 0)
    for tile in range(tiles):
        lanes = pl.ds(tile * LANES, LANES)
        rate = [row(mine, modes + 2 * SUBS + m, lanes) for m in range(modes)]
        decay = [jnp.exp(-r) for r in rate]
        state = [jnp.exp(rate[m] * sub.astype(F32) * (-float(span))) * row(entry, m, lanes) for m in range(modes)]
        more = [row(entry, modes + i, lanes) for i in range(4)]

        def pair(index, held, more=None):
            at = pl.ds(pl.multiple_of(index * 2 * SUBS, 2 * SUBS), 2 * SUBS)
            query, value = (part.astype(F32) for part in read(at, lanes))
            for half in range(2):
                v, q = value[half * SUBS : (half + 1) * SUBS], query[half * SUBS : (half + 1) * SUBS]
                if more is not None:
                    v = v + jnp.where(sub == 0, more[half], 0.0)
                    q = q + jnp.where(sub == 0, more[2 + half], 0.0)
                token = 2 * index + half
                mixed[tile, pl.ds(token, SUBS, stride=span), :] = q * tree_sum(list(held) + [v])
                held = [decay[m] * held[m] for m in range(modes)]
            return held

        state = pair(0, state, more)
        lax.fori_loop(1, span // 2, pair, state, unroll=2)
    return jnp.concatenate([mixed[tile, :rows] for tile in range(tiles)], axis=1).astype(BF16)


def near_kernel(pack, mine, other, w_out, share, entry, mixed):
    me = lax.axis_index("ch")
    chip, core = jnp.right_shift(me, 1), jnp.bitwise_and(me, 1)
    width = pack.shape[2]
    part = mix(lambda at, lanes: (pack[0, at, lanes], pack[1, at, lanes]), mine, other, entry, mixed)
    for slot, column in enumerate((1 - core, core)):
        start = pl.multiple_of((2 * chip + column) * width, width)
        share[slot] = jnp.dot(part, w_out[:, pl.ds(start, width)], preferred_element_type=F32)


def far_kernel(pack, mine, other, share, kept, sent, entry, mixed):
    core = jnp.bitwise_and(lax.axis_index("ch"), 1)
    width = pack.shape[2]
    part = mix(lambda at, lanes: (pack[0, at, lanes], pack[1, at, lanes]), mine, other, entry, mixed)
    for slot, (target, column) in enumerate(((sent, 1 - core), (kept, core))):
        start = pl.multiple_of(column * width, width)
        total = share[slot] + jnp.dot(part, pack[2, pl.ds(start, width), :], preferred_element_type=F32)
        target[...] = total.astype(target.dtype)


def known_kernel(entry, fix, message, rates, extra, mine, *again):
    modes = rates.shape[0]
    rate = rates[...]
    weight = extra[:modes] * jnp.sqrt(rate)
    lead = jnp.sum(weight * jnp.exp(rate), axis=0, keepdims=True)
    pieces = (
        entry[...],
        jnp.concatenate([fix[...], jnp.zeros_like(fix)], axis=0),
        message[modes : modes + SUBS],
        rate,
        weight * jnp.exp(-rate),
        jnp.concatenate([extra[modes : modes + 1], lead, jnp.zeros((SUBS - 2, rate.shape[1]), F32)], axis=0),
    )
    for target in (mine, *again[:1]):
        at = 0
        for piece in pieces:
            target[at : at + piece.shape[0]] = piece
            at += piece.shape[0]
    for target in again[1:]:
        target[...] = message[...]


def join(first, second, rates, rows):
    modes = rates.shape[0]
    start = second[modes : modes + SUBS]
    end = first[modes + SUBS :]
    added = start[0:2] * end[2:4] + end[0:2] * (start[2:4] + end[2:4])
    entering = first[:modes] + jnp.exp(rates) * added[0:1] + jnp.exp(2.0 * rates) * added[1:2]
    state = jnp.exp(-rates * float(rows)) * entering + second[:modes]
    both = jnp.concatenate([state, first[modes : modes + SUBS], second[modes + SUBS :]], axis=0)
    return both, entering, jnp.concatenate([added, end[4:6]], axis=0)


def scan_blocks(held, rates, rows, steps, level):
    block = lax.axis_index("seq")
    rounds = lax.axis_size("seq").bit_length() - 1
    message, entry, fix = held

    def place(level):
        upper = jnp.bitwise_and(jnp.right_shift(block, level), 1) == 1
        ahead = jnp.bitwise_and(block, (1 << level) - 1)
        return upper, ahead

    def ordered(upper, mine, other):
        return jnp.where(upper, other, mine), jnp.where(upper, mine, other)

    def enter(level, entry, fix, entering, added):
        upper, ahead = place(level)
        decay = jnp.exp(-rates * (ahead.astype(F32) * float(rows)))
        entry = jnp.where(upper, entry + decay * entering, entry)
        return entry, jnp.where(jnp.logical_and(upper, ahead == 0), added, fix)

    for masks in steps:
        if level >= rounds:
            break
        others = [seq_swap(message, mask) for mask in masks]
        upper, _ = place(level)
        message, entering, added = join(*ordered(upper, message, others[0]), rates, rows << level)
        entry, fix = enter(level, entry, fix, entering, added)
        if len(masks) == 3:
            pair, _, _ = join(*ordered(upper, others[1], others[2]), rates, rows << level)
            upper, _ = place(level + 1)
            message, entering, added = join(*ordered(upper, message, pair), rates, rows << (level + 1))
            entry, fix = enter(level + 1, entry, fix, entering, added)
        level += 1 if len(masks) == 1 else 2
    return message, entry, fix


def body(tokens, norm_gain, w_in, short_filter, rates, residues, skip_gain, w_out):
    rows, width = tokens.shape
    channels = w_in.shape[2]
    modes = rates.shape[0]
    far = ch_swap(tokens, 2)
    side = ch_swap(tokens, 1)
    mine = (jnp.transpose(w_in, (1, 0, 2)), short_filter, rates)
    staged = (tokens, norm_gain.reshape(-1, LANES))
    for array in mine:
        staged += (array, ch_swap(array, 1))
    kept = (0, 1, *range(2, len(staged), 2))
    staged = pl.pallas_call(
        stage_kernel,
        out_shape=tuple(jax.ShapeDtypeStruct(staged[i].shape, staged[i].dtype) for i in kept),
        in_specs=[pl.BlockSpec(memory_space=pl.ANY)] * len(staged),
        out_specs=tuple(vmem_specs(len(kept))),
        scratch_shapes=[pltpu.SemaphoreType.DMA((len(kept),))],
        compiler_params=pltpu.CompilerParams(vmem_limit_bytes=STAGE_VMEM),
        name="stage",
    )(*staged)
    far, staged = lax.optimization_barrier((far, staged))
    own_v, gain_v, w_in_v, taps_v, rates_v = staged
    side_far = ch_swap(far, 1)
    queries, gated, message = pl.pallas_call(
        front_kernel,
        out_shape=(
            jax.ShapeDtypeStruct((rows, channels), F32),
            jax.ShapeDtypeStruct((rows, channels), F32),
            jax.ShapeDtypeStruct((modes + 2 * SUBS, channels), F32),
        ),
        in_specs=vmem_specs(8),
        out_specs=tuple(vmem_specs(3)),
        scratch_shapes=[pltpu.VMEM((3 * channels // LANES, rows + rows // SUBS + HALO, LANES), F32)],
        compiler_params=pltpu.CompilerParams(vmem_limit_bytes=FRONT_VMEM),
        cost_estimate=pl.CostEstimate(flops=1_000_000, bytes_accessed=1_000, transcendentals=0),
        name="front",
    )(own_v, far, side, side_far, gain_v, w_in_v, taps_v, rates_v)
    skip = skip_gain.reshape(1, channels)
    pack, extra, w_out_v = pl.pallas_call(
        scan_kernel,
        out_shape=(
            jax.ShapeDtypeStruct((3, rows, channels), BF16),
            jax.ShapeDtypeStruct((modes + SUBS, channels), F32),
            jax.ShapeDtypeStruct(w_out.shape, BF16),
        ),
        in_specs=vmem_specs(7) + [pl.BlockSpec(memory_space=pl.ANY)] * 2,
        out_specs=tuple(vmem_specs(3)),
        scratch_shapes=[pltpu.VMEM((rows, channels), F32), pltpu.SemaphoreType.DMA((3,))],
        compiler_params=pltpu.CompilerParams(vmem_limit_bytes=SCAN_VMEM),
        cost_estimate=pl.CostEstimate(flops=2_000_000_000, bytes_accessed=1_000_000, transcendentals=0),
        name="scan",
    )(queries, gated, rates_v, residues, ch_swap(residues, 1), skip, ch_swap(skip, 1), w_out, ch_swap(w_out, 1))
    held = (message, jnp.zeros_like(rates_v), jnp.zeros((4, channels), F32))
    held = scan_blocks(held, rates_v, rows, SCAN_FIRST[:1], 0)
    held, pack = lax.optimization_barrier((held, pack))
    pack_far = ch_swap(pack, 2)
    held = scan_blocks(held, rates_v, rows, SCAN_FIRST[1:], 1)
    row_shape = jax.ShapeDtypeStruct((3 * modes + 3 * SUBS, channels), F32)

    def known(*operands, copies=False):
        out_shape = (row_shape, row_shape, jax.ShapeDtypeStruct(message.shape, F32))[: 3 if copies else 1]
        return pl.pallas_call(
            known_kernel,
            out_shape=out_shape,
            in_specs=vmem_specs(5),
            out_specs=tuple(vmem_specs(len(out_shape))),
            compiler_params=pltpu.CompilerParams(vmem_limit_bytes=STAGE_VMEM),
            name="known",
        )(*operands, rates_v, extra)

    def later(_, now):
        message, _, mine, _ = now
        held = (message, mine[:modes], mine[modes : modes + 4])
        message, entry, fix = scan_blocks(held, rates_v, rows, SCAN_LATER, len(SCAN_FIRST))
        (mine,) = known(entry, fix, message)
        other = seq_swap(message, SCAN_LAST)
        other_far = seq_swap(message, SCAN_LAST, 1)
        return other, other_far, mine, ch_swap(mine, 2)

    once = jnp.minimum(lax.axis_index("seq") + 1, 1)
    message, entry, fix = held
    mine, mine_again, message_again = known(entry, fix, message, copies=True)
    now = lax.fori_loop(0, once, later, (message, message_again, mine, mine_again))
    (other, other_far, mine, mine_far), pack_far = lax.optimization_barrier((now, pack_far))
    scratch = [pltpu.VMEM((modes + SUBS, channels), F32), pltpu.VMEM((channels // LANES, rows + rows // SUBS, LANES), F32)]
    share = pl.pallas_call(
        near_kernel,
        out_shape=jax.ShapeDtypeStruct((2, rows, width), F32),
        in_specs=vmem_specs(4),
        out_specs=vmem_specs(1)[0],
        scratch_shapes=scratch,
        compiler_params=pltpu.CompilerParams(vmem_limit_bytes=BACK_VMEM),
        cost_estimate=pl.CostEstimate(flops=900_000_000, bytes_accessed=4_000_000, transcendentals=0),
        name="near",
    )(pack, mine, other, w_out_v)
    kept, sent = pl.pallas_call(
        far_kernel,
        out_shape=(
            jax.ShapeDtypeStruct((rows, width), F32),
            jax.ShapeDtypeStruct((rows, width), BF16),
        ),
        in_specs=vmem_specs(4),
        out_specs=tuple(vmem_specs(2)),
        scratch_shapes=scratch,
        compiler_params=pltpu.CompilerParams(vmem_limit_bytes=BACK_VMEM),
        cost_estimate=pl.CostEstimate(flops=900_000_000, bytes_accessed=4_000_000, transcendentals=0),
        name="far",
    )(pack_far, mine_far, other_far, share)
    return (kept + ch_swap(sent, 1).astype(F32)).astype(BF16)


def solution(mesh):
    return jax.shard_map(
        body,
        mesh=mesh,
        in_specs=(
            P("seq", "ch"),
            P(),
            P(None, None, "ch"),
            P(None, None, "ch"),
            P(None, "ch"),
            P(None, "ch"),
            P("ch"),
            P("ch", None),
        ),
        out_specs=P("seq", "ch"),
        check_vma=False,
    )
```
